256 devices in a mesh: group: 8 (over y, core), dev: 32 (over x, z).
Axes of the slice: x: 4, y: 4, z: 8, core: 2. Of those that a mesh axis runs over, the one named last changes fastest.
Arguments:
- features_in: bfloat16 [96, 262144], P(None, ('group', 'dev')), may hold values from -6 to 6
- occupancy: int32 [262144], P(('group', 'dev')), may hold values 0 or 1
- cotangent: bfloat16 [96, 262144], P(None, ('group', 'dev')), may hold values from -6 to 6
- kernel_one: bfloat16 [27, 96, 96], replicated, may hold values from -0.125 to 0.125
- kernel_two: bfloat16 [27, 96, 96], replicated, may hold values from -0.125 to 0.125
- neighbours: int32 [512, 27], P(('group', 'dev')), may hold values from -1 to 5, as said below
Outputs:
- features_out: bfloat16 [96, 262144], P(None, ('group', 'dev'))
- kernel_one_grad: float32 [27, 96, 96], replicated
- kernel_two_grad: float32 [27, 96, 96], replicated
The draws below stay inside these ranges and needn't reach their ends.
Inputs may be any that keep to these rules, and one draw needn't show every extreme that they name: `neighbours`: the blocks of a device sit at distinct places of a 4 by 4 grid in y and z; the device's dev index is its slab's x position in the region. Entry 13 of a block is its own index. Other entries are -1 where no block lies at that offset (always beyond the first and last device of a region), n < 2 for block n of the same device, 2 + n for block n of the device with dev index one lower, 4 + n for block n of the device with dev index one higher; only offsets with dx = -1 or 1 reach other devices. The relation is mutual: entry t of block a names block b exactly when entry 26 - t of b names a.
All inputs are finite; a program needn't handle non-finite values. No bound on the sum of `occupancy` on one device may be relied on, other than what follows from the above.
Results may differ from the reference program's by a relative error of at most 0.0049.
Values may be sent and summed in bfloat16 or wider, within the bound.
No kernel may reach another device: no remote copies, remote signals or barrier semaphores. Data moves between devices by JAX's collectives and lax.ppermute only.
A program may use at most 64 MiB of HBM per device.

```python
import jax
import jax.numpy as jnp
import numpy as np
from jax import lax

CH = 96
BLK = 2
PLACES = 16
GROUPS = 8
PEERS = 32
BLOCKS = 512
VOXELS = 262144


def draw_neighbours(key, part):
    keys = jax.random.split(jax.random.fold_in(key, 21), GROUPS * PEERS)
    perms = jax.vmap(lambda one_key: jax.random.permutation(one_key, PLACES))(keys)
    spots = perms.reshape(GROUPS, PEERS, PLACES)[:, :, :BLK].astype(jnp.int32)
    place_ids = jnp.arange(PLACES, dtype=jnp.int32)
    block_ids = jnp.arange(BLK, dtype=jnp.int32)
    hits = spots[:, :, :, None] == place_ids[None, None, None, :]
    owned = jnp.sum(jnp.where(hits, block_ids[None, None, :, None], 0), axis=2)
    index_at = jnp.where(jnp.any(hits, axis=2), owned, -1).astype(jnp.int32)
    empty_row = jnp.full((GROUPS, 1, PLACES), -1, jnp.int32)
    index_pad = jnp.concatenate([empty_row, index_at, empty_row], axis=1)
    coord_y = spots // 4
    coord_z = spots % 4
    entries = []
    for step_x in (-1, 0, 1):
        rows = index_pad[:, 1 + step_x:1 + step_x + PEERS, :]
        base = 0 if step_x == 0 else BLK if step_x < 0 else 2 * BLK
        for step_y in (-1, 0, 1):
            for step_z in (-1, 0, 1):
                target_y = coord_y + step_y
                target_z = coord_z + step_z
                inside = (target_y >= 0) & (target_y < 4) & (target_z >= 0) & (target_z < 4)
                place = jnp.clip(target_y, 0, 3) * 4 + jnp.clip(target_z, 0, 3)
                found = jnp.take_along_axis(rows, place, axis=2)
                entries.append(jnp.where(inside & (found >= 0), found + base, -1))
    stacked = jnp.stack(entries, axis=-1)
    return stacked.reshape(BLOCKS, 27).astype(jnp.int32)


def place_ends(values, rng, smallest, top_value):
    shape = values.shape
    spot = [jax.random.randint(jax.random.fold_in(rng, axis), (), 0, shape[axis]) for axis in range(len(shape))]
    values = values.at[tuple(spot)].set(smallest)
    longest = shape.index(max(shape))
    spot[longest] = (spot[longest] + 1) % shape[longest]
    return values.at[tuple(spot)].set(top_value)


def level_of(own_key, shape, cuts, smallest, high):
    level = 1.0
    for dim, shards_of in cuts:
        heights = jax.random.uniform(jax.random.fold_in(jax.random.fold_in(own_key, 6), dim), (shards_of,), jnp.float32, smallest / len(cuts), high / len(cuts))
        level = level * jnp.repeat(jnp.exp(heights), shape[dim] // shards_of).reshape((-1,) + (1,) * (len(shape) - 1 - dim))
    return level


def noise(rng, dims, scale, reach, cuts=(), kind=jnp.bfloat16):
    drawn = scale * jax.random.normal(rng, dims, jnp.float32)
    if cuts:
        drawn = drawn * level_of(rng, dims, cuts, -0.22, 0.18)
    return jnp.clip(drawn, -reach, reach).astype(kind)


def setup_inputs(seed: int = 0) -> dict:
    key_list = jax.random.split(jax.random.key(seed), 7)
    features_in = noise(key_list[0], (CH, VOXELS), 1.0, 6.0, ((1, 256),))
    occupancy = place_ends((jax.random.randint(key_list[1], (VOXELS,), 0, 5) < 3).astype(jnp.int32), jax.random.fold_in(key_list[1], 1), 0, 1)
    cotangent = noise(key_list[2], (CH, VOXELS), 1.0, 6.0, ((1, 256),))
    kernel_one = noise(key_list[3], (27, CH, CH), (27 * CH) ** -0.5, 0.125)
    kernel_two = noise(key_list[4], (27, CH, CH), (27 * CH) ** -0.5, 0.125)
    neighbours = draw_neighbours(jax.random.fold_in(key_list[6], 71), 0)
    return dict(features_in=features_in, occupancy=occupancy, cotangent=cotangent, kernel_one=kernel_one, kernel_two=kernel_two, neighbours=neighbours)


def pad_tables():
    cells = np.arange(1000)
    coord_x = cells // 100
    coord_y = cells // 10 % 10
    coord_z = cells % 10

    def side(coord):
        return np.where(coord == 0, -1, np.where(coord == 9, 1, 0))

    def inner(coord):
        return np.where(coord == 0, 7, np.where(coord == 9, 0, coord - 1))
    offset_of = (side(coord_x) + 1) * 9 + (side(coord_y) + 1) * 3 + (side(coord_z) + 1)
    voxel_of = inner(coord_x) * 64 + inner(coord_y) * 8 + inner(coord_z)
    return (offset_of.astype(np.int32), voxel_of.astype(np.int32))

def cube_window(cube, first, second, third, width):
    return cube[:, :, first:first + 8, second:second + 8, third:third + 8].reshape(width, -1)

def conv_forward(padded, kernel):
    width = padded.shape[0]
    cube = padded.reshape(width, -1, 10, 10, 10)
    total = None
    for first in range(3):
        for second in range(3):
            stacked = jnp.concatenate([cube_window(cube, first, second, third, width) for third in range(3)], axis=0)
            start = first * 9 + second * 3
            weights = kernel[start:start + 3].reshape(3 * width, width)
            term = lax.dot_general(weights, stacked, (((0,), (0,)), ((), ())), preferred_element_type=jnp.float32)
            total = term if total is None else total + term
    return total

def kernel_terms(padded, grad):
    width = padded.shape[0]
    cube = padded.reshape(width, -1, 10, 10, 10)
    pieces = []
    for first in range(3):
        for second in range(3):
            stacked = jnp.concatenate([cube_window(cube, first, second, third, width) for third in range(3)], axis=0)
            term = lax.dot_general(stacked, grad, (((1,), (1,)), ((), ())), preferred_element_type=jnp.float32)
            pieces.append(term.reshape(3, width, width))
    return jnp.concatenate(pieces, axis=0)

def conv_backward(padded, kernel):
    width = padded.shape[0]
    cube = padded.reshape(width, -1, 10, 10, 10)
    total = None
    for first in range(3):
        for second in range(3):
            stacked = jnp.concatenate([cube_window(cube, 2 - first, 2 - second, 2 - third, width) for third in range(3)], axis=0)
            start = first * 9 + second * 3
            weights = jnp.concatenate([kernel[start + third] for third in range(3)], axis=1)
            term = jnp.dot(weights, stacked, preferred_element_type=jnp.float32)
            total = term if total is None else total + term
    return total

def global_neighbours(neighbours):
    owner = (jnp.arange(BLOCKS, dtype=jnp.int32) // BLK)[:, None]
    here = owner * BLK + neighbours
    lower = (owner - 1) * BLK + neighbours - BLK
    upper = (owner + 1) * BLK + neighbours - 2 * BLK
    found = jnp.where(neighbours < BLK, here, jnp.where(neighbours < 2 * BLK, lower, upper))
    return jnp.where(neighbours < 0, BLOCKS, found).astype(jnp.int32)

def reference(features_in, occupancy, cotangent, kernel_one, kernel_two, neighbours):
    offset_np, voxel_np = pad_tables()
    offset_of = jnp.asarray(offset_np)
    voxel_of = jnp.asarray(voxel_np)
    devices = BLOCKS // BLK
    span = BLK * 512
    where_nb = global_neighbours(neighbours)
    mask = occupancy.astype(jnp.float32)[None, :]
    occupied = occupancy[None, :] > 0
    scale = float(VOXELS) ** (-0.5)
    device_ids = jnp.arange(devices, dtype=jnp.int32)

    def with_zero(values):
        return jnp.concatenate([values, jnp.zeros((CH, 512), values.dtype)], axis=1)

    def padded_at(table, device):
        rows = lax.dynamic_slice_in_dim(where_nb, device * BLK, BLK, 0)
        columns = rows[:, offset_of] * 512 + voxel_of[None, :]
        return jnp.take(table, columns.reshape(-1), axis=1)

    def spread(stacked):
        return jnp.transpose(stacked, (1, 0, 2)).reshape(CH, VOXELS)

    def forward(values, kernel):
        table = with_zero(values)
        return spread(lax.map(lambda device: conv_forward(padded_at(table, device), kernel), device_ids))

    def backward(values, kernel):
        table = with_zero(values)
        return spread(lax.map(lambda device: conv_backward(padded_at(table, device), kernel), device_ids))

    def kernel_grad(values, grad):
        table = with_zero(values)

        def one(device):
            piece = lax.dynamic_slice_in_dim(grad, device * span, span, 1)
            return kernel_terms(padded_at(table, device), piece)
        return scale * lax.optimization_barrier(jnp.sum(lax.map(one, device_ids), axis=0))
    a_zero = jnp.where(occupied, features_in, jnp.zeros_like(features_in))
    z_one = mask * forward(a_zero, kernel_one)
    a_one = jax.nn.silu(z_one).astype(jnp.bfloat16)
    features_out = (mask * forward(a_one, kernel_two)).astype(jnp.bfloat16)
    g_two = jnp.where(occupied, cotangent, jnp.zeros_like(cotangent))
    kernel_two_grad = kernel_grad(a_one, g_two)
    ga_one = mask * backward(g_two, kernel_two)
    sigma = jax.nn.sigmoid(z_one)
    gz_one = (ga_one * sigma * (1.0 + z_one * (1.0 - sigma))).astype(jnp.bfloat16)
    kernel_one_grad = kernel_grad(a_zero, gz_one)
    return (features_out, kernel_one_grad, kernel_two_grad)
```

```python
import jax
import jax.numpy as jnp
from jax import lax
from jax.experimental import pallas as pl
from jax.experimental.pallas import tpu as pltpu
from jax.sharding import PartitionSpec as P

CH = 96
PAIRS = [(dy, dz) for dy in (-1, 0, 1) for dz in (-1, 0, 1)]
K9 = 9 * CH
F32 = jnp.float32
BF16 = jnp.bfloat16
NN = (((1,), (0,)), ((), ()))
NT = (((1,), (1,)), ((), ()))
VMEM = pl.BlockSpec(memory_space=pltpu.VMEM)
SMEM = pl.BlockSpec(memory_space=pltpu.SMEM)
ROWS = 4096
PACKED = 1296
LIMIT = 48 * 1024 * 1024


def dot(a, b, dims=NN):
    return lax.dot_general(a, b, dims, preferred_element_type=F32)


def lanes_low(rows):
    return lax.broadcasted_iota(jnp.int32, (rows, 128), 1) < 64


def pair_planes(first, second):
    low = lanes_low(first.shape[0])
    even = jnp.where(low, first, pltpu.roll(second, 64, 1))
    odd = jnp.where(low, pltpu.roll(first, 64, 1), second)
    return even, odd


def to_planes(ref, x):
    first = ref[:, x * 64 : x * 64 + 128].astype(F32)
    second = ref[:, 512 + x * 64 : 640 + x * 64].astype(F32)
    return pair_planes(first, second)


def selection(nb_ref, face):
    base = {0: 0, -1: 2, 1: 4}[face]
    lane = lax.broadcasted_iota(jnp.int32, (1, 128), 1)
    source = lax.broadcasted_iota(jnp.int32, (128, 128), 0)
    y = (lane // 8) % 8
    z = lane % 8
    pieces = []
    for dy, dz in PAIRS:
        far_y = y + dy
        far_z = z + dz
        out_y = (far_y < 0) | (far_y > 7)
        out_z = (far_z < 0) | (far_z > 7)

        def entry(block):
            def at(sy, sz):
                return nb_ref[block, (face + 1) * 9 + (sy + 1) * 3 + sz + 1] - base

            return jnp.where(
                out_y,
                jnp.where(out_z, at(dy, dz), at(dy, 0)),
                jnp.where(out_z, at(0, dz), at(0, 0)),
            )

        found = jnp.where(lane < 64, entry(0), entry(1))
        column = found * 64 + (far_y & 7) * 8 + (far_z & 7)
        column = jnp.where(found < 0, -1, column)
        pieces.append(jnp.where(source == column, 1.0, 0.0).astype(BF16))
    return pieces


def rim_kernel(feat_ref, cot_ref, occ_ref, low_ref, high_ref):
    for x, pick, out_ref in ((0, 0, low_ref), (6, 1, high_ref)):
        mask = to_planes(occ_ref, x)[pick] > 0
        for row, ref in ((0, feat_ref), (CH, cot_ref)):
            plane = to_planes(ref, x)[pick]
            out_ref[row : row + CH, :] = jnp.where(mask, plane, 0.0).astype(BF16)


def prep_kernel(
    feat_ref, cot_ref, occ_ref, w1_ref, w2_ref, nb_ref,
    a_ref, g_ref, zp_ref, gp_ref, w1t_ref, wb_ref, w2t_ref, sel_ref, mask_ref,
    planes_ref,
):
    for x in range(0, 8, 2):
        masks = to_planes(occ_ref, x)
        for k in range(2):
            mask_ref[:, (x + k) * 128 : (x + k + 1) * 128] = masks[k]
        for row, ref in ((0, feat_ref), (CH, cot_ref)):
            both = to_planes(ref, x)
            for k in range(2):
                planes_ref[x + k, row : row + CH, :] = jnp.where(masks[k] > 0, both[k], 0.0).astype(BF16)
    for index, face in enumerate((-1, 0, 1)):
        for j, piece in enumerate(selection(nb_ref, face)):
            sel_ref[index, :, j * 128 : (j + 1) * 128] = piece
    stacked = planes_ref[...].reshape(8 * 2 * CH, 128)
    for j in range(9):
        spread = dot(stacked, sel_ref[1, :, j * 128 : (j + 1) * 128]).astype(BF16)
        for x in range(8):
            a_ref[j * CH : (j + 1) * CH, x * 128 : (x + 1) * 128] = spread[x * 2 * CH : x * 2 * CH + CH]
            g_ref[j * CH : (j + 1) * CH, x * 128 : (x + 1) * 128] = spread[x * 2 * CH + CH : (x + 1) * 2 * CH]
    for d in range(3):
        w1t_ref[d] = w1_ref[d * K9 : (d + 1) * K9, :].astype(F32).T.astype(BF16)
        w2t_ref[d] = w2_ref[d * K9 : (d + 1) * K9, :].astype(F32).T.astype(BF16)
        wb_ref[d] = jnp.concatenate(
            [w2_ref[(26 - d * 9 - j) * CH : (27 - d * 9 - j) * CH, :] for j in range(9)], axis=1
        )
    for w_ref, v_ref, out_ref in ((w1t_ref, a_ref, zp_ref), (wb_ref, g_ref, gp_ref)):
        out_ref[...] = dot(w_ref[1], v_ref[...])
        out_ref[:, 128:] += dot(w_ref[0], v_ref[:, :896])
        out_ref[:, :896] += dot(w_ref[2], v_ref[:, 128:])


def spread_rim(rim, sel_ref, index, rows):
    full = dot(rim, sel_ref[index]).astype(BF16)
    parts = []
    for r in range(0, rows, CH):
        parts.append(
            jnp.concatenate([full[r : r + CH, j * 128 : (j + 1) * 128] for j in range(9)], axis=0)
        )
    return parts


def main_kernel(
    a_ref, g_ref, zp_ref, gp_ref, w1t_ref, wb_ref, sel_ref, mask_ref, low_ref, high_ref,
    own_ref, send_ref, a1_ref, a1_low_ref, a1_high_ref,
    grad_ref, packed_ref,
):
    scale = 262144.0 ** -0.5
    a_low, g_low = spread_rim(low_ref[...], sel_ref, 0, 2 * CH)
    a_high, g_high = spread_rim(high_ref[...], sel_ref, 2, 2 * CH)

    def finish(partial_ref, w_ref, low, high):
        first = partial_ref[:, :128] + dot(w_ref[0], low)
        last = partial_ref[:, 896:] + dot(w_ref[2], high)
        return mask_ref[...] * jnp.concatenate([first, partial_ref[:, 128:896], last], axis=1)

    z = finish(zp_ref, w1t_ref, a_low, a_high)
    ga = finish(gp_ref, wb_ref, g_low, g_high)
    sigma = 1.0 / (1.0 + jnp.exp(-z))
    a1 = (z * sigma).astype(BF16)
    gz = (ga * sigma * (1.0 + z * (1.0 - sigma))).astype(BF16)
    a1_ref[...] = a1
    a1_low_ref[...] = a1[:, :128]
    a1_high_ref[...] = a1[:, 896:]

    def terms(v_ref, low, high, grad, start):
        zero = jnp.zeros((K9, 32), F32)

        def put(d, value):
            r = start + d * K9
            grad_ref[r : r + K9, :] = jnp.concatenate([value * scale, zero], axis=1)

        put(0, dot(v_ref[:, :896], grad[:, 128:], NT) + dot(low, grad[:, :128], NT))
        put(1, dot(v_ref[...], grad, NT))
        put(2, dot(v_ref[:, 128:], grad[:, :896], NT) + dot(high, grad[:, 896:], NT))

    terms(g_ref, g_low, g_high, a1, 27 * CH)
    terms(a_ref, a_low, a_high, gz, 0)
    spare = grad_ref[3 * PACKED :, :]
    lane = lax.broadcasted_iota(jnp.int32, (PACKED, 128), 1)
    for k in range(3):
        moved = pltpu.roll(spare, 96 - 32 * k, 1)
        packed_ref[k * PACKED : (k + 1) * PACKED, :] = jnp.where(
            lane < 96, grad_ref[k * PACKED : (k + 1) * PACKED, :], moved
        ).astype(BF16)
    packed_ref[3 * PACKED :, :] = jnp.zeros((ROWS - 3 * PACKED, 128), BF16)
    half = ROWS // 2
    core = lax.rem(lax.axis_index("group"), 2)
    own_ref[...] = packed_ref[pl.ds(pl.multiple_of(core * half, half), half), :]
    send_ref[...] = packed_ref[pl.ds(pl.multiple_of((1 - core) * half, half), half), :]


def out_kernel(a1_ref, low_ref, high_ref, sel_ref, w2t_ref, mask_ref, out_ref, v_ref, planes_ref):
    for x in range(8):
        planes_ref[x] = a1_ref[:, x * 128 : (x + 1) * 128]
    stacked = planes_ref[...].reshape(8 * CH, 128)
    for j in range(9):
        spread = dot(stacked, sel_ref[1, :, j * 128 : (j + 1) * 128]).astype(BF16)
        for x in range(8):
            v_ref[j * CH : (j + 1) * CH, (x + 1) * 128 : (x + 2) * 128] = spread[x * CH : (x + 1) * CH]
    v_ref[:, :128] = spread_rim(low_ref[...], sel_ref, 0, CH)[0]
    v_ref[:, 1152:] = spread_rim(high_ref[...], sel_ref, 2, CH)[0]
    total = dot(w2t_ref[0], v_ref[:, :1024])
    total += dot(w2t_ref[1], v_ref[:, 128:1152])
    total += dot(w2t_ref[2], v_ref[:, 256:])
    total = mask_ref[...] * total
    for x in range(0, 8, 2):
        even = total[:, x * 128 : (x + 1) * 128]
        odd = total[:, (x + 1) * 128 : (x + 2) * 128]
        first, second = pair_planes(even, odd)
        out_ref[:, x * 64 : x * 64 + 128] = first.astype(BF16)
        out_ref[:, 512 + x * 64 : 640 + x * 64] = second.astype(BF16)


def part_kernel(count, axis_of, *refs):
    arrived, rest = refs[: len(refs) - count - 1], refs[len(refs) - count - 1 :]
    outs, total_ref = rest[:count], rest[count]
    total = arrived[0][...].astype(F32)
    for ref in arrived[1:]:
        total += ref[...].astype(F32)
    rows = total.shape[0] // count
    total_ref[...] = total.astype(BF16)
    me = axis_of()
    for k in range(count):
        start = lax.rem(me + k, count) * rows
        outs[k][...] = total_ref[pl.ds(pl.multiple_of(start, rows), rows), :]


def total_kernel(count, axis_of, *refs):
    arrived, out_ref, slots_ref = refs[:count], refs[count], refs[count + 1]
    me = axis_of()
    for k in range(count):
        slots_ref[lax.rem(me + count - k, count)] = arrived[k][...]
    total = slots_ref[0].astype(F32)
    for k in range(1, count):
        total += slots_ref[k].astype(F32)
    out_ref[...] = total.astype(BF16)


def join_kernel(count, axis_of, *refs):
    arrived, out_ref = refs[:count], refs[count]
    rows = out_ref.shape[0] // count
    me = axis_of()
    for k in range(count):
        start = lax.rem(me + count - k, count) * rows
        out_ref[pl.ds(pl.multiple_of(start, rows), rows), :] = arrived[k][...]


def grads_kernel(own_ref, other_ref, one_ref, two_ref, packed_ref):
    half = ROWS // 2
    core = lax.rem(lax.axis_index("group"), 2)
    packed_ref[pl.ds(pl.multiple_of(core * half, half), half), :] = own_ref[...].astype(F32)
    packed_ref[pl.ds(pl.multiple_of((1 - core) * half, half), half), :] = other_ref[...].astype(F32)

    def put(block, value):
        if block < 27:
            one_ref[block] = value[:, :CH]
        else:
            wide = jnp.concatenate([value, jnp.zeros((32, 128), F32)], axis=0)
            two_ref[53 - block] = wide.T[:CH, :CH]

    lane = lax.broadcasted_iota(jnp.int32, (48, 128), 1)

    def piece(start):
        if start < 3 * PACKED:
            return packed_ref[start : start + 48, :]
        r = start - 3 * PACKED
        value = None
        for k in range(3):
            moved = pltpu.roll(packed_ref[k * PACKED + r : k * PACKED + r + 48, :], (32 + 32 * k) % 128, 1)
            value = moved if k == 0 else jnp.where(lane < 32 * k, value, moved)
        return value

    for block in range(54):
        put(block, jnp.concatenate([piece(block * 96), piece(block * 96 + 48)], axis=0))


def shape(dims, dtype=BF16):
    return jax.ShapeDtypeStruct(dims, dtype)


def call(kernel, outs, *args, scratch=(), smem=(), flops=0, name=None):
    return pl.pallas_call(
        kernel,
        out_shape=outs,
        in_specs=[SMEM if k in smem else VMEM for k in range(len(args))],
        out_specs=jax.tree.map(lambda _: VMEM, outs),
        scratch_shapes=scratch,
        compiler_params=pltpu.CompilerParams(vmem_limit_bytes=LIMIT),
        cost_estimate=pl.CostEstimate(flops=flops, bytes_accessed=1 << 20, transcendentals=0),
        name=name,
    )(*args)


def staged_sum(own, send):
    core_pairs = [(g, g ^ 1) for g in range(8)]

    def x_pairs(k):
        return [(x * 8 + z, (x + k) % 4 * 8 + z) for x in range(4) for z in range(8)]

    def y_pairs(k):
        return [(y * 2 + c, (y + k) % 4 * 2 + c) for y in range(4) for c in range(2)]

    def z_pairs(k):
        return [(x * 8 + z, x * 8 + (z + k) % 8) for x in range(4) for z in range(8)]

    def at_x():
        return lax.axis_index("dev") // 8

    def at_y():
        return lax.axis_index("group") // 2

    def at_z():
        return lax.rem(lax.axis_index("dev"), 8)

    def part(arrived, count, axis_of, name):
        rows = arrived[0].shape[0]
        return call(
            lambda *refs: part_kernel(count, axis_of, *refs),
            [shape((rows // count, 128))] * count,
            *arrived,
            scratch=[pltpu.VMEM((rows, 128), BF16)],
            name=name,
        )

    def join(arrived, count, axis_of, name):
        return call(
            lambda *refs: join_kernel(count, axis_of, *refs),
            shape((arrived[0].shape[0] * count, 128)),
            *arrived,
            name=name,
        )

    got = lax.ppermute(send, "group", core_pairs)
    parts = part([own, got], 4, at_x, "sum_core")
    arrived = [parts[0]] + [lax.ppermute(parts[k], "dev", x_pairs(k)) for k in range(1, 4)]
    parts = part(arrived, 4, at_y, "sum_x")
    arrived = [parts[0]] + [lax.ppermute(parts[k], "group", y_pairs(k)) for k in range(1, 4)]
    (mine,) = part(arrived, 1, at_y, "sum_y")
    arrived = [mine] + [lax.ppermute(mine, "dev", z_pairs(k)) for k in range(1, 8)]
    mine = call(
        lambda *refs: total_kernel(8, at_z, *refs),
        shape(mine.shape),
        *arrived,
        scratch=[pltpu.VMEM((8,) + mine.shape, BF16)],
        name="sum_z",
    )
    arrived = [mine] + [lax.ppermute(mine, "group", y_pairs(k)) for k in range(1, 4)]
    mine = join(arrived, 4, at_y, "join_y")
    arrived = [mine] + [lax.ppermute(mine, "dev", x_pairs(k)) for k in range(1, 4)]
    mine = join(arrived, 4, at_x, "join_x")
    return mine, lax.ppermute(mine, "group", core_pairs)


def dev_shift(value, step):
    count = lax.axis_size("dev")
    pairs = [(i, i + step) for i in range(count) if 0 <= i + step < count]
    return lax.ppermute(value, "dev", pairs)


def per_device(features_in, occupancy, cotangent, kernel_one, kernel_two, neighbours):
    occ = occupancy.reshape(1, 1024)
    w1 = kernel_one.reshape(27 * CH, CH)
    w2 = kernel_two.reshape(27 * CH, CH)
    low, high = call(
        rim_kernel, [shape((2 * CH, 128))] * 2, features_in, cotangent, occ, name="rims"
    )
    upper = dev_shift(low, -1)
    lower = dev_shift(high, 1)
    a, g, zp, gp, w1t, wb, w2t, sel, mask = call(
        prep_kernel,
        [
            shape((K9, 1024)), shape((K9, 1024)), shape((CH, 1024), F32), shape((CH, 1024), F32),
            shape((3, CH, K9)), shape((3, CH, K9)), shape((3, CH, K9)),
            shape((3, 128, 1152)), shape((1, 1024), F32),
        ],
        features_in, cotangent, occ, w1, w2, neighbours,
        scratch=[pltpu.VMEM((8, 2 * CH, 128), BF16)],
        smem=(5,),
        flops=4 << 30,
        name="prep",
    )
    own, send, a1, a1_low, a1_high = call(
        main_kernel,
        [
            shape((ROWS // 2, 128)), shape((ROWS // 2, 128)), shape((CH, 1024)),
            shape((CH, 128)), shape((CH, 128)),
        ],
        a, g, zp, gp, w1t, wb, sel, mask, lower, upper,
        scratch=[pltpu.VMEM((54 * CH, 128), F32), pltpu.VMEM((ROWS, 128), BF16)],
        flops=4 << 30,
        name="gradients",
    )
    a1_upper = dev_shift(a1_low, -1)
    a1_lower = dev_shift(a1_high, 1)
    features_out = call(
        out_kernel,
        shape((CH, 1024)),
        a1, a1_lower, a1_upper, sel, w2t, mask,
        scratch=[pltpu.VMEM((K9, 1280), BF16), pltpu.VMEM((8, CH, 128), BF16)],
        flops=4 << 30,
        name="features",
    )
    mine, other = staged_sum(own, send)
    kernel_one_grad, kernel_two_grad = call(
        grads_kernel,
        [shape((27, CH, CH), F32)] * 2,
        mine, other,
        scratch=[pltpu.VMEM((ROWS, 128), F32)],
        name="unpack",
    )
    return (features_out, kernel_one_grad, kernel_two_grad)


def solution(mesh):
    return jax.shard_map(
        per_device,
        mesh=mesh,
        in_specs=(
            P(None, ("group", "dev")),
            P(("group", "dev")),
            P(None, ("group", "dev")),
            P(),
            P(),
            P(("group", "dev"), None),
        ),
        out_specs=(P(None, ("group", "dev")), P(), P()),
        check_vma=False,
    )
```

```python
import jax
import jax.numpy as jnp
from jax import lax
from jax.experimental import pallas as pl
from jax.experimental.pallas import tpu as pltpu
from jax.sharding import PartitionSpec as P

CH = 96
PAIRS = [(dy, dz) for dy in (-1, 0, 1) for dz in (-1, 0, 1)]
K9 = 9 * CH
F32 = jnp.float32
BF16 = jnp.bfloat16
NN = (((1,), (0,)), ((), ()))
NT = (((1,), (1,)), ((), ()))
VMEM = pl.BlockSpec(memory_space=pltpu.VMEM)
SMEM = pl.BlockSpec(memory_space=pltpu.SMEM)
ANY = pl.BlockSpec(memory_space=pl.ANY)
HBM = pl.BlockSpec(memory_space=pltpu.HBM)
BOTH = ("group", "dev")
ROWS = 4096
HALF = ROWS // 2
PACKED = 648
AROUND = 32
INPUTS = [pltpu.VMEM((CH, 1024), BF16), pltpu.VMEM((CH, 1024), BF16), pltpu.VMEM((1, 1024), jnp.int32)]


def dot(a, b, dims=NN):
    return lax.dot_general(a, b, dims, preferred_element_type=F32)


def lanes_low(rows):
    return lax.broadcasted_iota(jnp.int32, (rows, 128), 1) < 64


def pair_planes(first, second):
    low = lanes_low(first.shape[0])
    even = jnp.where(low, first, pltpu.roll(second, 64, 1))
    odd = jnp.where(low, pltpu.roll(first, 64, 1), second)
    return even, odd


def to_planes(ref, x):
    first = ref[:, x * 64 : x * 64 + 128].astype(F32)
    second = ref[:, 512 + x * 64 : 640 + x * 64].astype(F32)
    return pair_planes(first, second)


def selection(nb_ref, face):
    base = {0: 0, -1: 2, 1: 4}[face]
    lane = lax.broadcasted_iota(jnp.int32, (1, 128), 1)
    source = lax.broadcasted_iota(jnp.int32, (128, 128), 0)
    y = (lane // 8) % 8
    z = lane % 8
    pieces = []
    for dy, dz in PAIRS:
        far_y = y + dy
        far_z = z + dz
        out_y = (far_y < 0) | (far_y > 7)
        out_z = (far_z < 0) | (far_z > 7)

        def entry(block):
            def at(sy, sz):
                return nb_ref[block, (face + 1) * 9 + (sy + 1) * 3 + sz + 1] - base

            return jnp.where(
                out_y,
                jnp.where(out_z, at(dy, dz), at(dy, 0)),
                jnp.where(out_z, at(0, dz), at(0, 0)),
            )

        found = jnp.where(lane < 64, entry(0), entry(1))
        column = found * 64 + (far_y & 7) * 8 + (far_z & 7)
        column = jnp.where(found < 0, -1, column)
        pieces.append(jnp.where(source == column, 1.0, 0.0).astype(BF16))
    return pieces


def fetch(sources, targets, sems):
    copies = [
        pltpu.make_async_copy(source, target, sems.at[k])
        for k, (source, target) in enumerate(zip(sources, targets))
    ]
    for copy in copies:
        copy.start()
    return copies


def rim_kernel(feat_hbm, cot_hbm, occ_hbm, low_ref, high_ref, feat_ref, cot_ref, occ_ref, sems):
    for copy in fetch((feat_hbm, cot_hbm, occ_hbm), (feat_ref, cot_ref, occ_ref), sems):
        copy.wait()
    for x, pick, out_ref in ((0, 0, low_ref), (6, 1, high_ref)):
        mask = to_planes(occ_ref, x)[pick] > 0
        for row, ref in ((0, feat_ref), (CH, cot_ref)):
            plane = to_planes(ref, x)[pick]
            out_ref[row : row + CH, :] = jnp.where(mask, plane, 0.0).astype(BF16)


def turned(w_ref, d):
    return w_ref[d * K9 : (d + 1) * K9, :].astype(F32).T.astype(BF16)


def prep_kernel(
    feat_hbm, cot_hbm, occ_hbm, w1_hbm, w2_hbm, nb_ref,
    a_ref, g_ref, zp_ref, gp_ref, w1t_ref, wb_ref, sel_ref, mask_ref,
    feat_ref, cot_ref, occ_ref, w1_ref, w2_ref, planes_ref, sems,
):
    copies = fetch(
        (occ_hbm, feat_hbm, cot_hbm, w1_hbm, w2_hbm), (occ_ref, feat_ref, cot_ref, w1_ref, w2_ref), sems
    )
    for index, face in enumerate((-1, 0, 1)):
        for j, piece in enumerate(selection(nb_ref, face)):
            sel_ref[index, :, j * 128 : (j + 1) * 128] = piece
    for copy in copies[:3]:
        copy.wait()
    for x in range(0, 8, 2):
        masks = to_planes(occ_ref, x)
        for k in range(2):
            mask_ref[:, (x + k) * 128 : (x + k + 1) * 128] = masks[k]
        for row, ref in ((0, feat_ref), (CH, cot_ref)):
            both = to_planes(ref, x)
            for k in range(2):
                planes_ref[x + k, row : row + CH, :] = jnp.where(masks[k] > 0, both[k], 0.0).astype(BF16)
    stacked = planes_ref[...].reshape(8 * 2 * CH, 128)
    for j in range(9):
        spread = dot(stacked, sel_ref[1, :, j * 128 : (j + 1) * 128]).astype(BF16)
        for x in range(8):
            a_ref[j * CH : (j + 1) * CH, x * 128 : (x + 1) * 128] = spread[x * 2 * CH : x * 2 * CH + CH]
            g_ref[j * CH : (j + 1) * CH, x * 128 : (x + 1) * 128] = spread[x * 2 * CH + CH : (x + 1) * 2 * CH]
    for copy in copies[3:]:
        copy.wait()
    for d in range(3):
        w1t_ref[d] = turned(w1_ref, d)
        wb_ref[d] = jnp.concatenate(
            [w2_ref[(26 - d * 9 - j) * CH : (27 - d * 9 - j) * CH, :] for j in range(9)], axis=1
        )
    for w_ref, v_ref, out_ref in ((w1t_ref, a_ref, zp_ref), (wb_ref, g_ref, gp_ref)):
        out_ref[...] = dot(w_ref[1], v_ref[...])
        out_ref[:, 128:] += dot(w_ref[0], v_ref[:, :896])
        out_ref[:, :896] += dot(w_ref[2], v_ref[:, 128:])


def spread_rim(rim, sel_ref, index, rows):
    full = dot(rim, sel_ref[index]).astype(BF16)
    parts = []
    for r in range(0, rows, CH):
        parts.append(
            jnp.concatenate([full[r : r + CH, j * 128 : (j + 1) * 128] for j in range(9)], axis=0)
        )
    return parts


def main_kernel(
    a_ref, g_ref, zp_ref, gp_ref, w1t_ref, wb_ref, sel_ref, mask_ref, low_ref, high_ref,
    own_ref, send_ref, a1_ref, a1_low_ref, a1_high_ref,
    grad_ref, packed_ref,
):
    scale = 262144.0 ** -0.5
    a_low, g_low = spread_rim(low_ref[...], sel_ref, 0, 2 * CH)
    a_high, g_high = spread_rim(high_ref[...], sel_ref, 2, 2 * CH)

    def finish(partial_ref, w_ref, low, high):
        first = partial_ref[:, :128] + dot(w_ref[0], low)
        last = partial_ref[:, 896:] + dot(w_ref[2], high)
        return mask_ref[...] * jnp.concatenate([first, partial_ref[:, 128:896], last], axis=1)

    z = finish(zp_ref, w1t_ref, a_low, a_high)
    ga = finish(gp_ref, wb_ref, g_low, g_high)
    sigma = 1.0 / (1.0 + jnp.exp(-z))
    a1 = (z * sigma).astype(BF16)
    gz = (ga * sigma * (1.0 + z * (1.0 - sigma))).astype(BF16)
    a1_ref[...] = a1
    a1_low_ref[...] = a1[:, :128]
    a1_high_ref[...] = a1[:, 896:]

    def terms(v_ref, low, high, grad, start):
        zero = jnp.zeros((K9, 32), F32)

        def put(d, value):
            r = start + d * K9
            grad_ref[r : r + K9, :] = jnp.concatenate([value * scale, zero], axis=1)

        put(0, dot(v_ref[:, :896], grad[:, 128:], NT) + dot(low, grad[:, :128], NT))
        put(1, dot(v_ref[...], grad, NT))
        put(2, dot(v_ref[:, 128:], grad[:, :896], NT) + dot(high, grad[:, 896:], NT))

    terms(g_ref, g_low, g_high, a1, 27 * CH)
    terms(a_ref, a_low, a_high, gz, 0)
    lane = lax.broadcasted_iota(jnp.int32, (PACKED, 128), 1)
    for grad in range(2):
        rows = grad * 27 * CH
        base = grad * HALF
        spare = grad_ref[rows + 3 * PACKED : rows + 4 * PACKED, :]
        for k in range(3):
            kept = grad_ref[rows + k * PACKED : rows + (k + 1) * PACKED, :]
            packed_ref[base + k * PACKED : base + (k + 1) * PACKED, :] = jnp.where(
                lane < 96, kept, pltpu.roll(spare, 96 - 32 * k, 1)
            )
        packed_ref[base + 3 * PACKED : base + HALF, :] = jnp.zeros((HALF - 3 * PACKED, 128), F32)
    core = core_index()
    own_ref[...] = packed_ref[pl.ds(pl.multiple_of(core * HALF, HALF), HALF), :]
    send_ref[...] = packed_ref[pl.ds(pl.multiple_of((1 - core) * HALF, HALF), HALF), :].astype(BF16)


def out_kernel(a1_ref, low_ref, high_ref, sel_ref, w2_ref, mask_ref, after_ref, out_ref, v_ref, planes_ref):
    for x in range(8):
        planes_ref[x] = a1_ref[:, x * 128 : (x + 1) * 128]
    stacked = planes_ref[...].reshape(8 * CH, 128)
    for j in range(9):
        spread = dot(stacked, sel_ref[1, :, j * 128 : (j + 1) * 128]).astype(BF16)
        for x in range(8):
            v_ref[j * CH : (j + 1) * CH, (x + 1) * 128 : (x + 2) * 128] = spread[x * CH : (x + 1) * CH]
    v_ref[:, :128] = spread_rim(low_ref[...], sel_ref, 0, CH)[0]
    v_ref[:, 1152:] = spread_rim(high_ref[...], sel_ref, 2, CH)[0]
    total = dot(turned(w2_ref, 0), v_ref[:, :1024])
    total += dot(turned(w2_ref, 1), v_ref[:, 128:1152])
    total += dot(turned(w2_ref, 2), v_ref[:, 256:])
    total = mask_ref[...] * total
    for x in range(0, 8, 2):
        even = total[:, x * 128 : (x + 1) * 128]
        odd = total[:, (x + 1) * 128 : (x + 2) * 128]
        first, second = pair_planes(even, odd)
        out_ref[:, x * 64 : x * 64 + 128] = first.astype(BF16)
        out_ref[:, 512 + x * 64 : 640 + x * 64] = second.astype(BF16)


def core_index():
    return lax.rem(lax.axis_index("group"), 2)


def add_kernel(own_ref, got_ref, out_ref):
    out_ref[...] = (own_ref[...] + got_ref[...].astype(F32)).astype(BF16)


def rows_kernel(got_ref, low_ref, high_ref, out_ref):
    total = got_ref[0].astype(F32)
    for k in range(1, AROUND):
        total += got_ref[k].astype(F32)
    out_ref[...] = total.astype(BF16)


def total_kernel(*refs):
    out_ref, slots_ref = refs[-2:]
    me = lax.rem(lax.axis_index("dev"), 8) // 2
    for k in range(4):
        slots_ref[lax.rem(me + 4 - k, 4)] = refs[k][...]
    total = slots_ref[0].astype(F32)
    for k in range(1, 4):
        total += slots_ref[k].astype(F32)
    total = total.astype(BF16)
    for k in range(AROUND):
        out_ref[k] = total


def grads_kernel(own_ref, other_ref, one_hbm, two_hbm, packed_ref, one_ref, two_ref, sems):
    core = core_index()
    packed_ref[pl.ds(pl.multiple_of(core * HALF, HALF), HALF), :] = own_ref[...].astype(F32)
    packed_ref[pl.ds(pl.multiple_of((1 - core) * HALF, HALF), HALF), :] = other_ref[...].astype(F32)
    lane = lax.broadcasted_iota(jnp.int32, (24, 128), 1)

    def piece(grad, start):
        base = grad * HALF
        if start < 3 * PACKED:
            return packed_ref[base + start : base + start + 24, :]
        r = base + start - 3 * PACKED
        value = pltpu.roll(packed_ref[r : r + 24, :], 32, 1)
        for k in (1, 2):
            moved = pltpu.roll(packed_ref[r + k * PACKED : r + k * PACKED + 24, :], (32 + 32 * k) % 128, 1)
            value = jnp.where(lane < 32 * k, value, moved)
        return value

    def block_of(grad, block):
        return jnp.concatenate([piece(grad, block * CH + 24 * q) for q in range(4)], axis=0)

    copies = []
    for first in range(0, 27, 9):
        for block in range(first, first + 9):
            one_ref[block] = block_of(0, block)[:, :CH]
        part = pl.ds(first, 9)
        copies.append(pltpu.make_async_copy(one_ref.at[part], one_hbm.at[part], sems.at[len(copies)]))
        copies[-1].start()
    for first in range(18, -1, -9):
        for tap in range(first, first + 9):
            wide = jnp.concatenate([block_of(1, 26 - tap), jnp.zeros((32, 128), F32)], axis=0)
            two_ref[tap] = wide.T[:CH, :CH]
        part = pl.ds(first, 9)
        copies.append(pltpu.make_async_copy(two_ref.at[part], two_hbm.at[part], sems.at[len(copies)]))
        copies[-1].start()
    for copy in copies:
        copy.wait()


def shape(dims, dtype=BF16):
    return jax.ShapeDtypeStruct(dims, dtype)


def call(kernel, outs, *args, scratch=(), specs=None, out_specs=None, limit=8, flops=0, name=None):
    specs = specs or {}
    return pl.pallas_call(
        kernel,
        out_shape=outs,
        in_specs=[specs.get(k, VMEM) for k in range(len(args))],
        out_specs=out_specs or jax.tree.map(lambda _: VMEM, outs),
        scratch_shapes=scratch,
        compiler_params=pltpu.CompilerParams(vmem_limit_bytes=limit << 20),
        cost_estimate=pl.CostEstimate(flops=flops, bytes_accessed=1 << 20, transcendentals=0),
        name=name,
    )(*args)


def device_pairs(move):
    pairs = []
    for index in range(256):
        group, dev = index // 32, index % 32
        x, y, z, core = move(dev // 8, group // 2, dev % 8, group % 2)
        pairs.append((index, (y * 2 + core) * 32 + x * 8 + z))
    return pairs


def around_groups():
    return [
        [(y * 2 + core) * 32 + x * 8 + pair * 2 + z for y in range(4) for x in range(4) for z in range(2)]
        for core in range(2)
        for pair in range(4)
    ]


def all_to_all(value):
    return lax.all_to_all(value, BOTH, 0, 0, axis_index_groups=around_groups(), tiled=True)


def swap_core(value):
    return lax.ppermute(value, BOTH, device_pairs(lambda x, y, z, core: (x, y, z, 1 - core)))


def swap_z(value, k):
    return lax.ppermute(value, BOTH, device_pairs(lambda x, y, z, core: (x, y, (z + 2 * k) % 8, core)))


def dev_shift(value, step):
    count = lax.axis_size("dev")
    pairs = [(i, i + step) for i in range(count) if 0 <= i + step < count]
    return lax.ppermute(value, "dev", pairs)


def per_device(features_in, occupancy, cotangent, kernel_one, kernel_two, neighbours):
    occ = occupancy.reshape(1, 1024)
    w1 = kernel_one.reshape(27 * CH, CH)
    w2 = kernel_two.reshape(27 * CH, CH)
    low, high = call(
        rim_kernel,
        [shape((2 * CH, 128))] * 2,
        features_in, cotangent, occ,
        specs={0: HBM, 1: HBM, 2: HBM},
        scratch=INPUTS + [pltpu.SemaphoreType.DMA((3,))],
        name="rims",
    )
    upper = dev_shift(low, -1)
    lower = dev_shift(high, 1)
    a, g, zp, gp, w1t, wb, sel, mask = call(
        prep_kernel,
        [
            shape((K9, 1024)), shape((K9, 1024)), shape((CH, 1024), F32), shape((CH, 1024), F32),
            shape((3, CH, K9)), shape((3, CH, K9)), shape((3, 128, 1152)), shape((1, 1024), F32),
        ],
        features_in, cotangent, occ, w1, w2, neighbours,
        specs={0: HBM, 1: HBM, 2: HBM, 3: HBM, 4: HBM, 5: SMEM},
        scratch=INPUTS + [
            pltpu.VMEM((27 * CH, CH), BF16), pltpu.VMEM((27 * CH, CH), BF16),
            pltpu.VMEM((8, 2 * CH, 128), BF16), pltpu.SemaphoreType.DMA((5,)),
        ],
        limit=16,
        flops=4 << 30,
        name="prep",
    )
    own, send, a1, a1_low, a1_high = call(
        main_kernel,
        [
            shape((HALF, 128), F32), shape((HALF, 128)), shape((CH, 1024)),
            shape((CH, 128)), shape((CH, 128)),
        ],
        a, g, zp, gp, w1t, wb, sel, mask, lower, upper,
        scratch=[pltpu.VMEM((54 * CH, 128), F32), pltpu.VMEM((ROWS, 128), F32)],
        limit=16,
        flops=4 << 30,
        name="gradients",
    )
    got = swap_core(send)
    a1_upper = dev_shift(a1_low, -1)
    a1_lower = dev_shift(a1_high, 1)
    value = call(add_kernel, shape((HALF, 128)), own, got, name="sum_core")
    value = all_to_all(value.reshape(AROUND, HALF // AROUND, 128))
    value = call(
        rows_kernel, shape((HALF // AROUND, 128)), value, a1_lower, a1_upper,
        specs={1: ANY, 2: ANY}, name="sum_around",
    )
    arrived = [value] + [swap_z(value, k) for k in range(1, 4)]
    features_out = call(
        out_kernel,
        shape((CH, 1024)),
        a1, a1_lower, a1_upper, sel, w2, mask, value,
        specs={6: ANY},
        scratch=[pltpu.VMEM((K9, 1280), BF16), pltpu.VMEM((8, CH, 128), BF16)],
        limit=16,
        flops=4 << 30,
        name="features",
    )
    value = call(
        total_kernel, shape((AROUND, HALF // AROUND, 128)), *arrived, features_out,
        specs={4: ANY},
        scratch=[pltpu.VMEM((4, HALF // AROUND, 128), BF16)],
        name="sum_z",
    )
    mine = all_to_all(value).reshape(HALF, 128)
    kernel_one_grad, kernel_two_grad = call(
        grads_kernel,
        [shape((27, CH, CH), F32)] * 2,
        mine, swap_core(mine),
        out_specs=[HBM, HBM],
        scratch=[
            pltpu.VMEM((ROWS, 128), F32), pltpu.VMEM((27, CH, CH), F32), pltpu.VMEM((27, CH, CH), F32),
            pltpu.SemaphoreType.DMA((6,)),
        ],
        limit=16,
        name="unpack",
    )
    return (features_out, kernel_one_grad, kernel_two_grad)


def solution(mesh):
    return jax.shard_map(
        per_device,
        mesh=mesh,
        in_specs=(
            P(None, ("group", "dev")),
            P(("group", "dev")),
            P(None, ("group", "dev")),
            P(),
            P(),
            P(("group", "dev"), None),
        ),
        out_specs=(P(None, ("group", "dev")), P(), P()),
        check_vma=False,
    )
```

```python
import functools

import jax
import jax.numpy as jnp
from jax import lax
from jax.experimental import pallas as pl
from jax.experimental.pallas import tpu as pltpu
from jax.sharding import PartitionSpec as P

CH = 96
PAIRS = [(dy, dz) for dy in (-1, 0, 1) for dz in (-1, 0, 1)]
K9 = 9 * CH
F32 = jnp.float32
BF16 = jnp.bfloat16
NN = (((1,), (0,)), ((), ()))
NT = (((1,), (1,)), ((), ()))
VMEM = pl.BlockSpec(memory_space=pltpu.VMEM)
SMEM = pl.BlockSpec(memory_space=pltpu.SMEM)
ANY = pl.BlockSpec(memory_space=pl.ANY)
HBM = pl.BlockSpec(memory_space=pltpu.HBM)
BOTH = ("group", "dev")
ROWS = 4096
HALF = ROWS // 2
PACKED = 648
AROUND = 32
INPUTS = [pltpu.VMEM((CH, 1024), BF16), pltpu.VMEM((CH, 1024), BF16), pltpu.VMEM((1, 1024), jnp.int32)]


def dot(a, b, dims=NN):
    return lax.dot_general(a, b, dims, preferred_element_type=F32)


def lanes_low(rows):
    return lax.broadcasted_iota(jnp.int32, (rows, 128), 1) < 64


def pair_planes(first, second):
    low = lanes_low(first.shape[0])
    even = jnp.where(low, first, pltpu.roll(second, 64, 1))
    odd = jnp.where(low, pltpu.roll(first, 64, 1), second)
    return even, odd


def to_planes(ref, x):
    first = ref[:, x * 64 : x * 64 + 128].astype(F32)
    second = ref[:, 512 + x * 64 : 640 + x * 64].astype(F32)
    return pair_planes(first, second)


def selection(nb_ref, face):
    base = {0: 0, -1: 2, 1: 4}[face]
    lane = lax.broadcasted_iota(jnp.int32, (1, 128), 1)
    source = lax.broadcasted_iota(jnp.int32, (128, 128), 0)
    y = (lane // 8) % 8
    z = lane % 8
    pieces = []
    for dy, dz in PAIRS:
        far_y = y + dy
        far_z = z + dz
        out_y = (far_y < 0) | (far_y > 7)
        out_z = (far_z < 0) | (far_z > 7)

        def entry(block):
            def at(sy, sz):
                return nb_ref[block, (face + 1) * 9 + (sy + 1) * 3 + sz + 1] - base

            return jnp.where(
                out_y,
                jnp.where(out_z, at(dy, dz), at(dy, 0)),
                jnp.where(out_z, at(0, dz), at(0, 0)),
            )

        found = jnp.where(lane < 64, entry(0), entry(1))
        column = found * 64 + (far_y & 7) * 8 + (far_z & 7)
        column = jnp.where(found < 0, -1, column)
        pieces.append(jnp.where(source == column, 1.0, 0.0).astype(BF16))
    return pieces


def fetch(sources, targets, sems):
    copies = [
        pltpu.make_async_copy(source, target, sems.at[k])
        for k, (source, target) in enumerate(zip(sources, targets))
    ]
    for copy in copies:
        copy.start()
    return copies


def rim_kernel(feat_hbm, cot_hbm, occ_hbm, low_ref, high_ref, feat_ref, cot_ref, occ_ref, sems):
    for copy in fetch((feat_hbm, cot_hbm, occ_hbm), (feat_ref, cot_ref, occ_ref), sems):
        copy.wait()
    for x, pick, out_ref in ((0, 0, low_ref), (6, 1, high_ref)):
        mask = to_planes(occ_ref, x)[pick] > 0
        for row, ref in ((0, feat_ref), (CH, cot_ref)):
            plane = to_planes(ref, x)[pick]
            out_ref[row : row + CH, :] = jnp.where(mask, plane, 0.0).astype(BF16)


def turned(w_ref, d):
    return w_ref[d * K9 : (d + 1) * K9, :].astype(F32).T.astype(BF16)


def prep_kernel(
    feat_hbm, cot_hbm, occ_hbm, w1_hbm, w2_hbm, nb_hbm,
    v_ref, part_ref, w1t_ref, wb_ref, sel_ref, mask_ref,
    feat_ref, cot_ref, occ_ref, w1_ref, w2_ref, nb_ref, planes_ref, sems,
):
    copies = fetch(
        (nb_hbm, occ_hbm, feat_hbm, cot_hbm, w1_hbm, w2_hbm),
        (nb_ref, occ_ref, feat_ref, cot_ref, w1_ref, w2_ref),
        sems,
    )
    copies[0].wait()
    for index, face in enumerate((-1, 0, 1)):
        for j, piece in enumerate(selection(nb_ref, face)):
            sel_ref[index, :, j * 128 : (j + 1) * 128] = piece
    for copy in copies[1:4]:
        copy.wait()
    for x in range(0, 8, 2):
        masks = to_planes(occ_ref, x)
        for k in range(2):
            mask_ref[:, (x + k) * 128 : (x + k + 1) * 128] = masks[k]
        for row, ref in ((0, feat_ref), (CH, cot_ref)):
            both = to_planes(ref, x)
            for k in range(2):
                planes_ref[x + k, row : row + CH, :] = jnp.where(masks[k] > 0, both[k], 0.0).astype(BF16)
    stacked = planes_ref[...].reshape(8 * 2 * CH, 128)

    def place(j, spread):
        for x in range(8):
            for k in range(2):
                r = (x * 2 + k) * CH
                v_ref[k, j * CH : (j + 1) * CH, x * 128 : (x + 1) * 128] = spread[r : r + CH]

    spread_planes(stacked, sel_ref, place)
    for copy in copies[4:]:
        copy.wait()
    for d in range(3):
        w1t_ref[d] = turned(w1_ref, d)
        wb_ref[d] = jnp.concatenate(
            [w2_ref[(26 - d * 9 - j) * CH : (27 - d * 9 - j) * CH, :] for j in range(9)], axis=1
        )
    for k, w_ref in ((0, w1t_ref), (1, wb_ref)):
        part_ref[k] = dot(w_ref[1], v_ref[k])
        part_ref[k, :, 128:] += dot(w_ref[0], v_ref[k, :, :896])
        part_ref[k, :, :896] += dot(w_ref[2], v_ref[k, :, 128:])


def spread_planes(stacked, sel_ref, place):
    for j in range(0, 9, 2):
        wide = min(256, 1152 - j * 128)
        spread = dot(stacked, sel_ref[1, :, j * 128 : j * 128 + wide]).astype(BF16)
        for k in range(wide // 128):
            place(j + k, spread[:, k * 128 : (k + 1) * 128])


def spread_rim(rim, sel_ref, index, rows):
    full = dot(rim, sel_ref[index]).astype(BF16)
    parts = []
    for r in range(0, rows, CH):
        parts.append(
            jnp.concatenate([full[r : r + CH, j * 128 : (j + 1) * 128] for j in range(9)], axis=0)
        )
    return parts


def point_kernel(
    part_ref, w1t_ref, wb_ref, sel_ref, mask_ref, low_ref, high_ref,
    grad_ref, rim_ref, a1_low_ref, a1_high_ref,
):
    lows = spread_rim(low_ref[...], sel_ref, 0, 2 * CH)
    highs = spread_rim(high_ref[...], sel_ref, 2, 2 * CH)
    for k in range(2):
        rim_ref[k, 0] = lows[k]
        rim_ref[k, 1] = highs[k]

    def finish(k, w_ref):
        first = part_ref[k, :, :128] + dot(w_ref[0], lows[k])
        last = part_ref[k, :, 896:] + dot(w_ref[2], highs[k])
        return mask_ref[...] * jnp.concatenate([first, part_ref[k, :, 128:896], last], axis=1)

    z = finish(0, w1t_ref)
    sigma = 1.0 / (1.0 + jnp.exp(-z))
    a1 = (z * sigma).astype(BF16)
    grad_ref[1] = a1
    a1_low_ref[...] = a1[:, :128]
    a1_high_ref[...] = a1[:, 896:]
    ga = finish(1, wb_ref)
    grad_ref[0] = (ga * sigma * (1.0 + z * (1.0 - sigma))).astype(BF16)


def term_kernel(kept, v_ref, rim_ref, grad_ref, out_ref, terms_ref):
    which = core_index() if kept else 1 - core_index()
    grad = grad_ref[which]
    inner = v_ref[which]
    scale = 262144.0 ** -0.5
    zero = jnp.zeros((K9, 32), F32)
    views = (
        jnp.concatenate([rim_ref[which, 0], inner[:, :896]], axis=1),
        inner,
        jnp.concatenate([inner[:, 128:], rim_ref[which, 1]], axis=1),
    )
    for d, view in enumerate(views):
        value = dot(view, grad, NT) * scale
        terms_ref[d * K9 : (d + 1) * K9, :] = jnp.concatenate([value, zero], axis=1)
    lane = lax.broadcasted_iota(jnp.int32, (PACKED, 128), 1)
    spare = terms_ref[3 * PACKED : 4 * PACKED, :]
    for k in range(3):
        value = jnp.where(
            lane < 96, terms_ref[k * PACKED : (k + 1) * PACKED, :], pltpu.roll(spare, 96 - 32 * k, 1)
        )
        out_ref[k * PACKED : (k + 1) * PACKED, :] = value.astype(out_ref.dtype)
    out_ref[3 * PACKED : HALF, :] = jnp.zeros((HALF - 3 * PACKED, 128), out_ref.dtype)


def out_kernel(
    grad_ref, low_ref, high_ref, sel_ref, w2_hbm, mask_ref, after_ref, out_ref, w2_ref, v_ref, planes_ref, sems
):
    (copy,) = fetch((w2_hbm,), (w2_ref,), sems)
    for x in range(8):
        planes_ref[x] = grad_ref[1, :, x * 128 : (x + 1) * 128]

    def place(j, spread):
        for x in range(8):
            v_ref[j * CH : (j + 1) * CH, (x + 1) * 128 : (x + 2) * 128] = spread[x * CH : (x + 1) * CH]

    spread_planes(planes_ref[...].reshape(8 * CH, 128), sel_ref, place)
    v_ref[:, :128] = spread_rim(low_ref[...], sel_ref, 0, CH)[0]
    v_ref[:, 1152:] = spread_rim(high_ref[...], sel_ref, 2, CH)[0]
    copy.wait()
    total = dot(turned(w2_ref, 0), v_ref[:, :1024])
    total += dot(turned(w2_ref, 1), v_ref[:, 128:1152])
    total += dot(turned(w2_ref, 2), v_ref[:, 256:])
    total = mask_ref[...] * total
    for x in range(0, 8, 2):
        even = total[:, x * 128 : (x + 1) * 128]
        odd = total[:, (x + 1) * 128 : (x + 2) * 128]
        first, second = pair_planes(even, odd)
        out_ref[:, x * 64 : x * 64 + 128] = first.astype(BF16)
        out_ref[:, 512 + x * 64 : 640 + x * 64] = second.astype(BF16)


def core_index():
    return lax.rem(lax.axis_index("group"), 2)


def add_kernel(own_ref, got_ref, low_ref, high_ref, out_ref):
    out_ref[...] = (own_ref[...] + got_ref[...].astype(F32)).astype(BF16)


def rows_kernel(got_ref, after_ref, out_ref):
    total = got_ref[0].astype(F32)
    for k in range(1, AROUND):
        total += got_ref[k].astype(F32)
    out_ref[...] = total.astype(BF16)


def total_kernel(*refs):
    out_ref, slots_ref = refs[-2:]
    me = lax.rem(lax.axis_index("dev"), 8) // 2
    for k in range(4):
        slots_ref[lax.rem(me + 4 - k, 4)] = refs[k][...]
    total = slots_ref[0].astype(F32)
    for k in range(1, 4):
        total += slots_ref[k].astype(F32)
    total = total.astype(BF16)
    for k in range(AROUND):
        out_ref[k] = total


def grads_kernel(own_ref, other_ref, one_hbm, two_hbm, packed_ref, one_ref, two_ref, sems):
    core = core_index()
    packed_ref[pl.ds(pl.multiple_of(core * HALF, HALF), HALF), :] = own_ref[...].astype(F32)
    packed_ref[pl.ds(pl.multiple_of((1 - core) * HALF, HALF), HALF), :] = other_ref[...].astype(F32)
    lane = lax.broadcasted_iota(jnp.int32, (24, 128), 1)

    def piece(grad, start):
        base = grad * HALF
        if start < 3 * PACKED:
            return packed_ref[base + start : base + start + 24, :]
        r = base + start - 3 * PACKED
        value = pltpu.roll(packed_ref[r : r + 24, :], 32, 1)
        for k in (1, 2):
            moved = pltpu.roll(packed_ref[r + k * PACKED : r + k * PACKED + 24, :], (32 + 32 * k) % 128, 1)
            value = jnp.where(lane < 32 * k, value, moved)
        return value

    def block_of(grad, block):
        return jnp.concatenate([piece(grad, block * CH + 24 * q) for q in range(4)], axis=0)

    copies = []
    for first in range(0, 27, 9):
        for block in range(first, first + 9):
            one_ref[block] = block_of(0, block)[:, :CH]
        part = pl.ds(first, 9)
        copies.append(pltpu.make_async_copy(one_ref.at[part], one_hbm.at[part], sems.at[len(copies)]))
        copies[-1].start()
    for first in range(18, -1, -9):
        for tap in range(first, first + 9):
            wide = jnp.concatenate([block_of(1, 26 - tap), jnp.zeros((32, 128), F32)], axis=0)
            two_ref[tap] = wide.T[:CH, :CH]
        part = pl.ds(first, 9)
        copies.append(pltpu.make_async_copy(two_ref.at[part], two_hbm.at[part], sems.at[len(copies)]))
        copies[-1].start()
    for copy in copies:
        copy.wait()


def shape(dims, dtype=BF16):
    return jax.ShapeDtypeStruct(dims, dtype)


def call(kernel, outs, *args, scratch=(), specs=None, out_specs=None, limit=8, flops=0, name=None):
    specs = specs or {}
    return pl.pallas_call(
        kernel,
        out_shape=outs,
        in_specs=[specs.get(k, VMEM) for k in range(len(args))],
        out_specs=out_specs or jax.tree.map(lambda _: VMEM, outs),
        scratch_shapes=scratch,
        compiler_params=pltpu.CompilerParams(vmem_limit_bytes=limit << 20),
        cost_estimate=pl.CostEstimate(flops=flops, bytes_accessed=1 << 20, transcendentals=0),
        name=name,
    )(*args)


def device_pairs(move):
    pairs = []
    for index in range(256):
        group, dev = index // 32, index % 32
        x, y, z, core = move(dev // 8, group // 2, dev % 8, group % 2)
        pairs.append((index, (y * 2 + core) * 32 + x * 8 + z))
    return pairs


def around_groups():
    return [
        [(y * 2 + core) * 32 + x * 8 + pair * 2 + z for y in range(4) for x in range(4) for z in range(2)]
        for core in range(2)
        for pair in range(4)
    ]


def all_to_all(value):
    return lax.all_to_all(value, BOTH, 0, 0, axis_index_groups=around_groups(), tiled=True)


def swap_core(value):
    return lax.ppermute(value, BOTH, device_pairs(lambda x, y, z, core: (x, y, z, 1 - core)))


def swap_z(value, k):
    return lax.ppermute(value, BOTH, device_pairs(lambda x, y, z, core: (x, y, (z + 2 * k) % 8, core)))


def dev_shift(value, step):
    count = lax.axis_size("dev")
    pairs = [(i, i + step) for i in range(count) if 0 <= i + step < count]
    return lax.ppermute(value, "dev", pairs)


def in_hbm(value):
    return pltpu.with_memory_space_constraint(value, pltpu.HBM)


def per_device(features_in, occupancy, cotangent, kernel_one, kernel_two, neighbours):
    features_in = in_hbm(features_in)
    cotangent = in_hbm(cotangent)
    occ = in_hbm(occupancy.reshape(1, 1024))
    w1 = in_hbm(kernel_one.reshape(27 * CH, CH))
    w2 = in_hbm(kernel_two.reshape(27 * CH, CH))
    neighbours = in_hbm(neighbours)
    low, high = call(
        rim_kernel,
        [shape((2 * CH, 128))] * 2,
        features_in, cotangent, occ,
        specs={0: HBM, 1: HBM, 2: HBM},
        scratch=INPUTS + [pltpu.SemaphoreType.DMA((3,))],
        name="rims",
    )
    upper = dev_shift(low, -1)
    lower = dev_shift(high, 1)
    v, part, w1t, wb, sel, mask = call(
        prep_kernel,
        [
            shape((2, K9, 1024)), shape((2, CH, 1024), F32),
            shape((3, CH, K9)), shape((3, CH, K9)), shape((3, 128, 1152)), shape((1, 1024), F32),
        ],
        features_in, cotangent, occ, w1, w2, neighbours,
        specs={k: HBM for k in range(6)},
        scratch=INPUTS + [
            pltpu.VMEM((27 * CH, CH), BF16), pltpu.VMEM((27 * CH, CH), BF16), pltpu.SMEM((2, 27), jnp.int32),
            pltpu.VMEM((8, 2 * CH, 128), BF16), pltpu.SemaphoreType.DMA((6,)),
        ],
        limit=16,
        flops=4 << 30,
        name="prep",
    )
    grad, rim, a1_low, a1_high = call(
        point_kernel,
        [shape((2, CH, 1024)), shape((2, 2, K9, 128)), shape((CH, 128)), shape((CH, 128))],
        part, w1t, wb, sel, mask, lower, upper,
        limit=16,
        flops=1 << 30,
        name="points",
    )
    a1_upper = dev_shift(a1_low, -1)
    a1_lower = dev_shift(a1_high, 1)

    def terms(kept):
        return call(
            functools.partial(term_kernel, kept),
            shape((HALF, 128), F32 if kept else BF16),
            v, rim, grad,
            scratch=[pltpu.VMEM((27 * CH, 128), F32)],
            limit=16,
            flops=2 << 30,
            name="terms_kept" if kept else "terms_sent",
        )

    got = swap_core(terms(False))
    value = call(
        add_kernel, shape((HALF, 128)), terms(True), got, a1_lower, a1_upper,
        specs={2: ANY, 3: ANY}, name="sum_core",
    )
    moved = all_to_all(value.reshape(AROUND, HALF // AROUND, 128))
    features_out = call(
        out_kernel,
        shape((CH, 1024)),
        grad, a1_lower, a1_upper, sel, w2, mask, in_hbm(value),
        specs={4: HBM, 6: HBM},
        scratch=[
            pltpu.VMEM((27 * CH, CH), BF16), pltpu.VMEM((K9, 1280), BF16), pltpu.VMEM((8, CH, 128), BF16),
            pltpu.SemaphoreType.DMA((1,)),
        ],
        limit=16,
        flops=3 << 30,
        name="features",
    )
    value = call(
        rows_kernel, shape((HALF // AROUND, 128)), moved, in_hbm(features_out),
        specs={1: HBM}, name="sum_around",
    )
    arrived = [value] + [swap_z(value, k) for k in range(1, 4)]
    value = call(
        total_kernel, shape((AROUND, HALF // AROUND, 128)), *arrived,
        scratch=[pltpu.VMEM((4, HALF // AROUND, 128), BF16)],
        name="sum_z",
    )
    mine = all_to_all(value).reshape(HALF, 128)
    kernel_one_grad, kernel_two_grad = call(
        grads_kernel,
        [shape((27, CH, CH), F32)] * 2,
        mine, swap_core(mine),
        out_specs=[HBM, HBM],
        scratch=[
            pltpu.VMEM((ROWS, 128), F32), pltpu.VMEM((27, CH, CH), F32), pltpu.VMEM((27, CH, CH), F32),
            pltpu.SemaphoreType.DMA((6,)),
        ],
        limit=16,
        name="unpack",
    )
    return (features_out, kernel_one_grad, kernel_two_grad)


def solution(mesh):
    return jax.shard_map(
        per_device,
        mesh=mesh,
        in_specs=(
            P(None, ("group", "dev")),
            P(("group", "dev")),
            P(None, ("group", "dev")),
            P(),
            P(),
            P(("group", "dev"), None),
        ),
        out_specs=(P(None, ("group", "dev")), P(), P()),
        check_vma=False,
    )
```

```python
import functools

import jax
import jax.numpy as jnp
from jax import lax
from jax.experimental import pallas as pl
from jax.experimental.pallas import tpu as pltpu
from jax.sharding import PartitionSpec as P

CH = 96
PAIRS = [(dy, dz) for dy in (-1, 0, 1) for dz in (-1, 0, 1)]
K9 = 9 * CH
F32 = jnp.float32
BF16 = jnp.bfloat16
NN = (((1,), (0,)), ((), ()))
NT = (((1,), (1,)), ((), ()))
VMEM = pl.BlockSpec(memory_space=pltpu.VMEM)
SMEM = pl.BlockSpec(memory_space=pltpu.SMEM)
ANY = pl.BlockSpec(memory_space=pl.ANY)
HBM = pl.BlockSpec(memory_space=pltpu.HBM)
BOTH = ("group", "dev")
ROWS = 4096
HALF = ROWS // 2
AROUND = 32
INPUTS = [pltpu.VMEM((CH, 1024), BF16), pltpu.VMEM((CH, 1024), BF16), pltpu.VMEM((1, 1024), jnp.int32)]


def dot(a, b, dims=NN):
    return lax.dot_general(a, b, dims, preferred_element_type=F32)


def lanes_low(rows):
    return lax.broadcasted_iota(jnp.int32, (rows, 128), 1) < 64


def pair_planes(first, second):
    low = lanes_low(first.shape[0])
    even = jnp.where(low, first, pltpu.roll(second, 64, 1))
    odd = jnp.where(low, pltpu.roll(first, 64, 1), second)
    return even, odd


def to_planes(ref, x):
    first = ref[:, x * 64 : x * 64 + 128].astype(F32)
    second = ref[:, 512 + x * 64 : 640 + x * 64].astype(F32)
    return pair_planes(first, second)


def source_lanes(nb_ref, face):
    base = {0: 0, -1: 2, 1: 4}[face]
    lane = lax.broadcasted_iota(jnp.int32, (1, 128), 1)
    y = (lane // 8) % 8
    z = lane % 8
    rows = []
    for dy, dz in PAIRS:
        far_y = y + dy
        far_z = z + dz
        out_y = (far_y < 0) | (far_y > 7)
        out_z = (far_z < 0) | (far_z > 7)

        def entry(block):
            def at(sy, sz):
                return nb_ref[block, (face + 1) * 9 + (sy + 1) * 3 + sz + 1] - base

            return jnp.where(
                out_y,
                jnp.where(out_z, at(dy, dz), at(dy, 0)),
                jnp.where(out_z, at(0, dz), at(0, 0)),
            )

        found = jnp.where(lane < 64, entry(0), entry(1))
        column = found * 64 + (far_y & 7) * 8 + (far_z & 7)
        rows.append(jnp.where(found < 0, -1, column).astype(F32))
    return rows


def selection(rows):
    source = lax.broadcasted_iota(jnp.int32, (128, 128), 0).astype(F32)
    return jnp.concatenate([jnp.where(source == row, 1.0, 0.0).astype(BF16) for row in rows], axis=1)


def fetch(sources, targets, sems):
    copies = [
        pltpu.make_async_copy(source, target, sems.at[k])
        for k, (source, target) in enumerate(zip(sources, targets))
    ]
    for copy in copies:
        copy.start()
    return copies


def rim_kernel(
    feat_hbm, cot_hbm, occ_hbm, nb_hbm, low_ref, high_ref, feat_ref, cot_ref, occ_ref, nb_ref, sems
):
    copies = fetch((nb_hbm, occ_hbm, feat_hbm, cot_hbm), (nb_ref, occ_ref, feat_ref, cot_ref), sems)
    copies[0].wait()
    inner = source_lanes(nb_ref, 0)
    sides = [inner + source_lanes(nb_ref, face) for face in (-1, 1)]
    for copy in copies[1:]:
        copy.wait()
    for x, edge, rows, out_ref in ((0, 0, sides[0], low_ref), (6, 1, sides[1], high_ref)):
        masks = to_planes(occ_ref, x)
        planes = [jnp.where(m > 0, p, 0.0) for m, p in zip(masks, to_planes(feat_ref, x))]
        out_ref[:CH, :] = planes[edge].astype(BF16)
        out_ref[CH : 2 * CH, :] = jnp.where(masks[edge] > 0, to_planes(cot_ref, x)[edge], 0.0).astype(BF16)
        out_ref[2 * CH : 3 * CH, :] = planes[1 - edge].astype(BF16)
        table = jnp.concatenate([masks[edge]] + rows + [jnp.zeros((13, 128), F32)], axis=0)
        out_ref[3 * CH :, :] = table.astype(BF16)


def turned(w_ref, d):
    return w_ref[d * K9 : (d + 1) * K9, :].astype(F32).T.astype(BF16)


def prep_kernel(
    feat_hbm, cot_hbm, occ_hbm, w1_hbm, w2_hbm, nb_hbm,
    v_ref, part_ref, w1t_ref, wb_ref, sel_ref, mask_ref,
    feat_ref, cot_ref, occ_ref, w1_ref, w2_ref, nb_ref, planes_ref, sems,
):
    copies = fetch(
        (nb_hbm, occ_hbm, feat_hbm, cot_hbm, w1_hbm, w2_hbm),
        (nb_ref, occ_ref, feat_ref, cot_ref, w1_ref, w2_ref),
        sems,
    )
    copies[0].wait()
    for index, face in enumerate((-1, 0, 1)):
        sel_ref[index] = selection(source_lanes(nb_ref, face))
    for copy in copies[1:4]:
        copy.wait()
    for x in range(0, 8, 2):
        masks = to_planes(occ_ref, x)
        for k in range(2):
            mask_ref[:, (x + k) * 128 : (x + k + 1) * 128] = masks[k]
        for row, ref in ((0, feat_ref), (CH, cot_ref)):
            both = to_planes(ref, x)
            for k in range(2):
                planes_ref[x + k, row : row + CH, :] = jnp.where(masks[k] > 0, both[k], 0.0).astype(BF16)
    stacked = planes_ref[...].reshape(8 * 2 * CH, 128)

    def place(j, spread):
        for x in range(8):
            for k in range(2):
                r = (x * 2 + k) * CH
                v_ref[k, j * CH : (j + 1) * CH, x * 128 : (x + 1) * 128] = spread[r : r + CH]

    spread_planes(stacked, sel_ref, place)
    for copy in copies[4:]:
        copy.wait()
    for d in range(3):
        w1t_ref[d * CH : (d + 1) * CH, :] = turned(w1_ref, d)
        wb_ref[d * CH : (d + 1) * CH, :] = jnp.concatenate(
            [w2_ref[(26 - d * 9 - j) * CH : (27 - d * 9 - j) * CH, :] for j in range(9)], axis=1
        )
    for k, w_ref in ((0, w1t_ref), (1, wb_ref)):
        full = dot(w_ref[...], v_ref[k])
        part_ref[k] = full[CH : 2 * CH]
        part_ref[k, :, 128:] += full[:CH, :896]
        part_ref[k, :, :896] += full[2 * CH :, 128:]


def spread_planes(stacked, sel_ref, place):
    for j in range(0, 9, 2):
        wide = min(256, 1152 - j * 128)
        spread = dot(stacked, sel_ref[1, :, j * 128 : j * 128 + wide]).astype(BF16)
        for k in range(wide // 128):
            place(j + k, spread[:, k * 128 : (k + 1) * 128])


def spread_rim(rim, select):
    full = dot(rim, select).astype(BF16)
    return [
        jnp.concatenate([full[r : r + CH, j * 128 : (j + 1) * 128] for j in range(9)], axis=0)
        for r in range(0, rim.shape[0], CH)
    ]


def point_kernel(part_ref, w1t_ref, wb_ref, sel_ref, mask_ref, low_ref, high_ref, grad_ref, rim_ref):
    lows = spread_rim(low_ref[: 2 * CH, :], sel_ref[0])
    highs = spread_rim(high_ref[: 2 * CH, :], sel_ref[2])
    for k in range(2):
        rim_ref[k, :, :128] = lows[k]
        rim_ref[k, :, 128:] = highs[k]

    def finish(k, w_ref):
        first = part_ref[k, :, :128] + dot(w_ref[:CH, :], lows[k])
        last = part_ref[k, :, 896:] + dot(w_ref[2 * CH :, :], highs[k])
        return mask_ref[...] * jnp.concatenate([first, part_ref[k, :, 128:896], last], axis=1)

    z = finish(0, w1t_ref)
    sigma = 1.0 / (1.0 + jnp.exp(-z))
    grad_ref[1] = (z * sigma).astype(BF16)
    ga = finish(1, wb_ref)
    grad_ref[0] = (ga * sigma * (1.0 + z * (1.0 - sigma))).astype(BF16)


def term_kernel(kept, v_ref, rim_ref, grad_ref, out_ref):
    which = core_index() if kept else 1 - core_index()
    grad = grad_ref[which]
    gap = jnp.zeros((CH, 128), BF16)
    inner = jnp.concatenate(
        [
            jnp.concatenate([grad[:, 128:], gap], axis=1),
            grad,
            jnp.concatenate([gap, grad[:, :896]], axis=1),
        ],
        axis=0,
    )
    sides = jnp.concatenate(
        [
            jnp.concatenate([grad[:, :128], gap], axis=1),
            jnp.concatenate([gap, gap], axis=1),
            jnp.concatenate([gap, grad[:, 896:]], axis=1),
        ],
        axis=0,
    )
    value = (dot(inner, v_ref[which], NT) + dot(sides, rim_ref[which], NT)) * (262144.0 ** -0.5)
    value = jnp.concatenate([value, jnp.zeros((3 * CH, 32), F32)], axis=1).astype(out_ref.dtype)
    for k in range(7):
        out_ref[k * 3 * CH : (k + 1) * 3 * CH, :] = value[:, k * 128 : (k + 1) * 128]
    out_ref[21 * CH :, :] = jnp.zeros((HALF - 21 * CH, 128), out_ref.dtype)


def beside(payload_ref, own, below, w1t_ref):
    table = payload_ref[3 * CH :, :].astype(F32)
    inner = selection([table[1 + j : 2 + j] for j in range(9)])
    across = selection([table[10 + j : 11 + j] for j in range(9)])
    (edge,) = spread_rim(payload_ref[:CH, :], inner)
    (far,) = spread_rim(payload_ref[2 * CH : 3 * CH, :], inner)
    (near,) = spread_rim(own, across)
    before, after = (far, near) if below else (near, far)
    z = dot(w1t_ref[:CH, :], before) + dot(w1t_ref[CH : 2 * CH, :], edge) + dot(w1t_ref[2 * CH :, :], after)
    z = table[:1] * z
    return (z / (1.0 + jnp.exp(-z))).astype(BF16)


def out_kernel(
    grad_ref, lower_ref, upper_ref, low_ref, high_ref, w1t_ref, sel_ref, w2_hbm, mask_ref, after_ref,
    out_ref, w2_ref, w2t_ref, v_ref, planes_ref, sems,
):
    (copy,) = fetch((w2_hbm,), (w2_ref,), sems)
    for x in range(8):
        planes_ref[x] = grad_ref[1, :, x * 128 : (x + 1) * 128]

    def place(j, spread):
        for x in range(8):
            v_ref[j * CH : (j + 1) * CH, (x + 1) * 128 : (x + 2) * 128] = spread[x * CH : (x + 1) * CH]

    spread_planes(planes_ref[...].reshape(8 * CH, 128), sel_ref, place)
    v_ref[:, :128] = spread_rim(beside(lower_ref, low_ref[:CH, :], True, w1t_ref), sel_ref[0])[0]
    v_ref[:, 1152:] = spread_rim(beside(upper_ref, high_ref[:CH, :], False, w1t_ref), sel_ref[2])[0]
    copy.wait()
    for d in range(3):
        w2t_ref[d * CH : (d + 1) * CH, :] = turned(w2_ref, d)
    full = dot(w2t_ref[...], v_ref[...])
    total = full[:CH, :1024] + full[CH : 2 * CH, 128:1152] + full[2 * CH :, 256:]
    total = mask_ref[...] * total
    for x in range(0, 8, 2):
        even = total[:, x * 128 : (x + 1) * 128]
        odd = total[:, (x + 1) * 128 : (x + 2) * 128]
        first, second = pair_planes(even, odd)
        out_ref[:, x * 64 : x * 64 + 128] = first.astype(BF16)
        out_ref[:, 512 + x * 64 : 640 + x * 64] = second.astype(BF16)


def core_index():
    return lax.rem(lax.axis_index("group"), 2)


def add_kernel(own_ref, got_ref, out_ref):
    out_ref[...] = (own_ref[...] + got_ref[...].astype(F32)).astype(BF16)


def rows_kernel(got_ref, after_ref, out_ref):
    total = got_ref[0].astype(F32)
    for k in range(1, AROUND):
        total += got_ref[k].astype(F32)
    out_ref[...] = total.astype(BF16)


def total_kernel(*refs):
    out_ref, slots_ref = refs[-2:]
    me = lax.rem(lax.axis_index("dev"), 8) // 2
    for k in range(4):
        slots_ref[lax.rem(me + 4 - k, 4)] = refs[k][...]
    total = slots_ref[0].astype(F32)
    for k in range(1, 4):
        total += slots_ref[k].astype(F32)
    total = total.astype(BF16)
    for k in range(AROUND):
        out_ref[k] = total


def grads_kernel(own_ref, other_ref, one_hbm, two_hbm, packed_ref, one_ref, two_ref, sems):
    core = core_index()
    packed_ref[pl.ds(pl.multiple_of(core * HALF, HALF), HALF), :] = own_ref[...].astype(F32)
    packed_ref[pl.ds(pl.multiple_of((1 - core) * HALF, HALF), HALF), :] = other_ref[...].astype(F32)
    lane = lax.broadcasted_iota(jnp.int32, (CH, 128), 1)

    def block_of(grad, block):
        d, j = block // 9, block % 9
        at, off = j * CH // 128, j * CH % 128
        row = grad * HALF + at * 3 * CH + d * CH
        value = packed_ref[row : row + CH, :]
        if off == 0:
            return value
        value = pltpu.roll(value, 128 - off, 1)
        if off > 32:
            more = pltpu.roll(packed_ref[row + 3 * CH : row + 4 * CH, :], 128 - off, 1)
            value = jnp.where(lane < 128 - off, value, more)
        return value

    copies = []

    def flush(ref, hbm, first):
        part = pl.ds(first, 9)
        copies.append(pltpu.make_async_copy(ref.at[part], hbm.at[part], sems.at[len(copies)]))
        copies[-1].start()

    for first in range(18, -1, -9):
        for tap in range(first, first + 9):
            two_ref[tap] = block_of(1, 26 - tap)[:, :CH]
        flush(two_ref, two_hbm, first)
    for first in range(0, 27, 9):
        for tap in range(first, first + 9):
            wide = jnp.concatenate([block_of(0, tap), jnp.zeros((32, 128), F32)], axis=0)
            one_ref[tap] = wide.T[:CH, :CH]
        flush(one_ref, one_hbm, first)
    for copy in copies:
        copy.wait()


def shape(dims, dtype=BF16):
    return jax.ShapeDtypeStruct(dims, dtype)


def call(kernel, outs, *args, scratch=(), specs=None, out_specs=None, limit=8, flops=0, name=None):
    specs = specs or {}
    return pl.pallas_call(
        kernel,
        out_shape=outs,
        in_specs=[specs.get(k, VMEM) for k in range(len(args))],
        out_specs=out_specs or jax.tree.map(lambda _: VMEM, outs),
        scratch_shapes=scratch,
        compiler_params=pltpu.CompilerParams(vmem_limit_bytes=limit << 20),
        cost_estimate=pl.CostEstimate(flops=flops, bytes_accessed=1 << 20, transcendentals=0),
        name=name,
    )(*args)


def device_pairs(move):
    pairs = []
    for index in range(256):
        group, dev = index // 32, index % 32
        x, y, z, core = move(dev // 8, group // 2, dev % 8, group % 2)
        pairs.append((index, (y * 2 + core) * 32 + x * 8 + z))
    return pairs


def around_groups():
    return [
        [(y * 2 + core) * 32 + x * 8 + pair * 2 + z for y in range(4) for x in range(4) for z in range(2)]
        for core in range(2)
        for pair in range(4)
    ]


def all_to_all(value):
    return lax.all_to_all(value, BOTH, 0, 0, axis_index_groups=around_groups(), tiled=True)


def swap_core(value):
    return lax.ppermute(value, BOTH, device_pairs(lambda x, y, z, core: (x, y, z, 1 - core)))


def swap_z(value, k):
    return lax.ppermute(value, BOTH, device_pairs(lambda x, y, z, core: (x, y, (z + 2 * k) % 8, core)))


def dev_shift(value, step):
    count = lax.axis_size("dev")
    pairs = [(i, i + step) for i in range(count) if 0 <= i + step < count]
    return lax.ppermute(value, "dev", pairs)


def in_hbm(value):
    return pltpu.with_memory_space_constraint(value, pltpu.HBM)


def per_device(features_in, occupancy, cotangent, kernel_one, kernel_two, neighbours):
    features_in = in_hbm(features_in)
    cotangent = in_hbm(cotangent)
    occ = in_hbm(occupancy.reshape(1, 1024))
    w1 = in_hbm(kernel_one.reshape(27 * CH, CH))
    w2 = in_hbm(kernel_two.reshape(27 * CH, CH))
    neighbours = in_hbm(neighbours)
    low, high = call(
        rim_kernel,
        [shape((3 * CH + 32, 128))] * 2,
        features_in, cotangent, occ, neighbours,
        specs={k: HBM for k in range(4)},
        scratch=INPUTS + [pltpu.SMEM((2, 27), jnp.int32), pltpu.SemaphoreType.DMA((4,))],
        name="rims",
    )
    upper = dev_shift(low, -1)
    lower = dev_shift(high, 1)
    v, part, w1t, wb, sel, mask = call(
        prep_kernel,
        [
            shape((2, K9, 1024)), shape((2, CH, 1024), F32),
            shape((3 * CH, K9)), shape((3 * CH, K9)), shape((3, 128, 1152)), shape((1, 1024), F32),
        ],
        features_in, cotangent, occ, w1, w2, neighbours,
        specs={k: HBM for k in range(6)},
        scratch=INPUTS + [
            pltpu.VMEM((27 * CH, CH), BF16), pltpu.VMEM((27 * CH, CH), BF16), pltpu.SMEM((2, 27), jnp.int32),
            pltpu.VMEM((8, 2 * CH, 128), BF16), pltpu.SemaphoreType.DMA((6,)),
        ],
        limit=16,
        flops=4 << 30,
        name="prep",
    )
    grad, rim = call(
        point_kernel,
        [shape((2, CH, 1024)), shape((2, K9, 256))],
        part, w1t, wb, sel, mask, lower, upper,
        limit=16,
        flops=1 << 30,
        name="points",
    )

    def terms(kept):
        return call(
            functools.partial(term_kernel, kept),
            shape((HALF, 128), F32 if kept else BF16),
            v, rim, grad,
            limit=16,
            flops=2 << 30,
            name="terms_kept" if kept else "terms_sent",
        )

    got = swap_core(terms(False))
    value = call(add_kernel, shape((HALF, 128)), terms(True), got, name="sum_core")
    moved = all_to_all(value.reshape(AROUND, HALF // AROUND, 128))
    features_out = call(
        out_kernel,
        shape((CH, 1024)),
        grad, lower, upper, low, high, w1t, sel, w2, mask, in_hbm(value),
        specs={7: HBM, 9: HBM},
        scratch=[
            pltpu.VMEM((27 * CH, CH), BF16), pltpu.VMEM((3 * CH, K9), BF16),
            pltpu.VMEM((K9, 1280), BF16), pltpu.VMEM((8, CH, 128), BF16),
            pltpu.SemaphoreType.DMA((1,)),
        ],
        limit=16,
        flops=3 << 30,
        name="features",
    )
    value = call(
        rows_kernel, shape((HALF // AROUND, 128)), moved, in_hbm(features_out),
        specs={1: HBM}, name="sum_around",
    )
    arrived = [value] + [swap_z(value, k) for k in range(1, 4)]
    value = call(
        total_kernel, shape((AROUND, HALF // AROUND, 128)), *arrived,
        scratch=[pltpu.VMEM((4, HALF // AROUND, 128), BF16)],
        name="sum_z",
    )
    mine = all_to_all(value).reshape(HALF, 128)
    kernel_one_grad, kernel_two_grad = call(
        grads_kernel,
        [shape((27, CH, CH), F32)] * 2,
        mine, swap_core(mine),
        out_specs=[HBM, HBM],
        scratch=[
            pltpu.VMEM((ROWS, 128), F32), pltpu.VMEM((27, CH, CH), F32), pltpu.VMEM((27, CH, CH), F32),
            pltpu.SemaphoreType.DMA((6,)),
        ],
        limit=16,
        name="unpack",
    )
    return (features_out, kernel_one_grad, kernel_two_grad)


def solution(mesh):
    return jax.shard_map(
        per_device,
        mesh=mesh,
        in_specs=(
            P(None, ("group", "dev")),
            P(("group", "dev")),
            P(None, ("group", "dev")),
            P(),
            P(),
            P(("group", "dev"), None),
        ),
        out_specs=(P(None, ("group", "dev")), P(), P()),
        check_vma=False,
    )
```

```python
import functools

import jax
import jax.numpy as jnp
from jax import lax
from jax.experimental import pallas as pl
from jax.experimental.pallas import tpu as pltpu
from jax.sharding import PartitionSpec as P

CH = 96
PAIRS = [(dy, dz) for dy in (-1, 0, 1) for dz in (-1, 0, 1)]
K9 = 9 * CH
F32 = jnp.float32
BF16 = jnp.bfloat16
NN = (((1,), (0,)), ((), ()))
NT = (((1,), (1,)), ((), ()))
VMEM = pl.BlockSpec(memory_space=pltpu.VMEM)
SMEM = pl.BlockSpec(memory_space=pltpu.SMEM)
ANY = pl.BlockSpec(memory_space=pl.ANY)
HBM = pl.BlockSpec(memory_space=pltpu.HBM)
BOTH = ("group", "dev")
ROWS = 4096
HALF = ROWS // 2
AROUND = 32
INPUTS = [pltpu.VMEM((CH, 1024), BF16), pltpu.VMEM((CH, 1024), BF16), pltpu.VMEM((1, 1024), jnp.int32)]


def dot(a, b, dims=NN):
    return lax.dot_general(a, b, dims, preferred_element_type=F32)


def lanes_low(rows):
    return lax.broadcasted_iota(jnp.int32, (rows, 128), 1) < 64


def pair_planes(first, second):
    low = lanes_low(first.shape[0])
    even = jnp.where(low, first, pltpu.roll(second, 64, 1))
    odd = jnp.where(low, pltpu.roll(first, 64, 1), second)
    return even, odd


def to_planes(ref, x):
    first = ref[:, x * 64 : x * 64 + 128].astype(F32)
    second = ref[:, 512 + x * 64 : 640 + x * 64].astype(F32)
    return pair_planes(first, second)


def source_lanes(nb_ref, face):
    base = {0: 0, -1: 2, 1: 4}[face]
    lane = lax.broadcasted_iota(jnp.int32, (1, 128), 1)
    y = (lane // 8) % 8
    z = lane % 8
    rows = []
    for dy, dz in PAIRS:
        far_y = y + dy
        far_z = z + dz
        out_y = (far_y < 0) | (far_y > 7)
        out_z = (far_z < 0) | (far_z > 7)

        def entry(block):
            def at(sy, sz):
                return nb_ref[block, (face + 1) * 9 + (sy + 1) * 3 + sz + 1] - base

            return jnp.where(
                out_y,
                jnp.where(out_z, at(dy, dz), at(dy, 0)),
                jnp.where(out_z, at(0, dz), at(0, 0)),
            )

        found = jnp.where(lane < 64, entry(0), entry(1))
        column = found * 64 + (far_y & 7) * 8 + (far_z & 7)
        rows.append(jnp.where(found < 0, -1, column).astype(F32))
    return rows


def selection(rows):
    source = lax.broadcasted_iota(jnp.int32, (128, 128), 0).astype(F32)
    return jnp.concatenate([jnp.where(source == row, 1.0, 0.0).astype(BF16) for row in rows], axis=1)


def fetch(sources, targets, sems):
    copies = [
        pltpu.make_async_copy(source, target, sems.at[k])
        for k, (source, target) in enumerate(zip(sources, targets))
    ]
    for copy in copies:
        copy.start()
    return copies


def rim_kernel(
    feat_hbm, cot_hbm, occ_hbm, nb_hbm, first_ref, second_ref, feat_ref, cot_ref, occ_ref, nb_ref, both_ref, sems
):
    copies = fetch((nb_hbm, occ_hbm, feat_hbm, cot_hbm), (nb_ref, occ_ref, feat_ref, cot_ref), sems)
    copies[0].wait()
    inner = source_lanes(nb_ref, 0)
    sides = [inner + source_lanes(nb_ref, face) for face in (-1, 1)]
    for copy in copies[1:]:
        copy.wait()
    for x, edge, rows in ((0, 0, sides[0]), (6, 1, sides[1])):
        out_ref = both_ref.at[edge]
        masks = to_planes(occ_ref, x)
        planes = [jnp.where(m > 0, p, 0.0) for m, p in zip(masks, to_planes(feat_ref, x))]
        out_ref[:CH, :] = planes[edge].astype(BF16)
        out_ref[CH : 2 * CH, :] = jnp.where(masks[edge] > 0, to_planes(cot_ref, x)[edge], 0.0).astype(BF16)
        out_ref[2 * CH : 3 * CH, :] = planes[1 - edge].astype(BF16)
        table = jnp.concatenate([masks[edge]] + rows + [jnp.zeros((13, 128), F32)], axis=0)
        out_ref[3 * CH :, :] = table.astype(BF16)
    odd = dev_parity()
    first_ref[...] = both_ref[1 - odd]
    second_ref[...] = both_ref[odd]


def dev_parity():
    return lax.rem(lax.axis_index("dev"), 2)


def lower_upper(first_ref, second_ref, both_ref):
    both_ref[0] = first_ref[...]
    both_ref[1] = second_ref[...]
    odd = dev_parity()
    return both_ref.at[1 - odd], both_ref.at[odd]


def turned(w_ref, d):
    return w_ref[d * K9 : (d + 1) * K9, :].astype(F32).T.astype(BF16)


def prep_kernel(
    feat_hbm, cot_hbm, occ_hbm, w1_hbm, w2_hbm, nb_hbm,
    v_ref, part_ref, w1t_ref, wb_ref, sel_ref, mask_ref,
    feat_ref, cot_ref, occ_ref, w1_ref, w2_ref, nb_ref, planes_ref, sems,
):
    copies = fetch(
        (nb_hbm, occ_hbm, feat_hbm, cot_hbm, w1_hbm, w2_hbm),
        (nb_ref, occ_ref, feat_ref, cot_ref, w1_ref, w2_ref),
        sems,
    )
    copies[0].wait()
    for index, face in enumerate((-1, 0, 1)):
        sel_ref[index] = selection(source_lanes(nb_ref, face))
    for copy in copies[1:4]:
        copy.wait()
    for x in range(0, 8, 2):
        masks = to_planes(occ_ref, x)
        for k in range(2):
            mask_ref[:, (x + k) * 128 : (x + k + 1) * 128] = masks[k]
        for row, ref in ((0, feat_ref), (CH, cot_ref)):
            both = to_planes(ref, x)
            for k in range(2):
                planes_ref[x + k, row : row + CH, :] = jnp.where(masks[k] > 0, both[k], 0.0).astype(BF16)
    stacked = planes_ref[...].reshape(8 * 2 * CH, 128)

    def place(j, spread):
        for x in range(8):
            for k in range(2):
                r = (x * 2 + k) * CH
                v_ref[k, j * CH : (j + 1) * CH, x * 128 : (x + 1) * 128] = spread[r : r + CH]

    spread_planes(stacked, sel_ref, place)
    for copy in copies[4:]:
        copy.wait()
    for d in range(3):
        w1t_ref[d * CH : (d + 1) * CH, :] = turned(w1_ref, d)
        wb_ref[d * CH : (d + 1) * CH, :] = jnp.concatenate(
            [w2_ref[(26 - d * 9 - j) * CH : (27 - d * 9 - j) * CH, :] for j in range(9)], axis=1
        )
    for k, w_ref in ((0, w1t_ref), (1, wb_ref)):
        full = dot(w_ref[...], v_ref[k])
        part_ref[k] = full[CH : 2 * CH]
        part_ref[k, :, 128:] += full[:CH, :896]
        part_ref[k, :, :896] += full[2 * CH :, 128:]


def spread_planes(stacked, sel_ref, place):
    for j in range(0, 9, 2):
        wide = min(256, 1152 - j * 128)
        spread = dot(stacked, sel_ref[1, :, j * 128 : j * 128 + wide]).astype(BF16)
        for k in range(wide // 128):
            place(j + k, spread[:, k * 128 : (k + 1) * 128])


def spread_rim(rim, select):
    full = dot(rim, select).astype(BF16)
    return [
        jnp.concatenate([full[r : r + CH, j * 128 : (j + 1) * 128] for j in range(9)], axis=0)
        for r in range(0, rim.shape[0], CH)
    ]


def point_kernel(part_ref, w1t_ref, wb_ref, sel_ref, mask_ref, first_ref, second_ref, grad_ref, rim_ref, both_ref):
    low_ref, high_ref = lower_upper(first_ref, second_ref, both_ref)
    lows = spread_rim(low_ref[: 2 * CH, :], sel_ref[0])
    highs = spread_rim(high_ref[: 2 * CH, :], sel_ref[2])
    for k in range(2):
        rim_ref[k, :, :128] = lows[k]
        rim_ref[k, :, 128:] = highs[k]

    def finish(k, w_ref):
        first = part_ref[k, :, :128] + dot(w_ref[:CH, :], lows[k])
        last = part_ref[k, :, 896:] + dot(w_ref[2 * CH :, :], highs[k])
        return mask_ref[...] * jnp.concatenate([first, part_ref[k, :, 128:896], last], axis=1)

    z = finish(0, w1t_ref)
    sigma = 1.0 / (1.0 + jnp.exp(-z))
    grad_ref[1] = (z * sigma).astype(BF16)
    ga = finish(1, wb_ref)
    grad_ref[0] = (ga * sigma * (1.0 + z * (1.0 - sigma))).astype(BF16)


def term_kernel(kept, v_ref, rim_ref, grad_ref, out_ref):
    which = core_index() if kept else 1 - core_index()
    grad = grad_ref[which]
    gap = jnp.zeros((CH, 128), BF16)
    inner = jnp.concatenate(
        [
            jnp.concatenate([grad[:, 128:], gap], axis=1),
            grad,
            jnp.concatenate([gap, grad[:, :896]], axis=1),
        ],
        axis=0,
    )
    sides = jnp.concatenate(
        [
            jnp.concatenate([grad[:, :128], gap], axis=1),
            jnp.concatenate([gap, gap], axis=1),
            jnp.concatenate([gap, grad[:, 896:]], axis=1),
        ],
        axis=0,
    )
    value = (dot(inner, v_ref[which], NT) + dot(sides, rim_ref[which], NT)) * (262144.0 ** -0.5)
    value = jnp.concatenate([value, jnp.zeros((3 * CH, 32), F32)], axis=1).astype(out_ref.dtype)
    for k in range(7):
        out_ref[k * 3 * CH : (k + 1) * 3 * CH, :] = value[:, k * 128 : (k + 1) * 128]
    out_ref[21 * CH :, :] = jnp.zeros((HALF - 21 * CH, 128), out_ref.dtype)


def beside(payload_ref, own, below, w1t_ref):
    table = payload_ref[3 * CH :, :].astype(F32)
    inner = selection([table[1 + j : 2 + j] for j in range(9)])
    across = selection([table[10 + j : 11 + j] for j in range(9)])
    (edge,) = spread_rim(payload_ref[:CH, :], inner)
    (far,) = spread_rim(payload_ref[2 * CH : 3 * CH, :], inner)
    (near,) = spread_rim(own, across)
    before, after = (far, near) if below else (near, far)
    z = dot(w1t_ref[:CH, :], before) + dot(w1t_ref[CH : 2 * CH, :], edge) + dot(w1t_ref[2 * CH :, :], after)
    z = table[:1] * z
    return (z / (1.0 + jnp.exp(-z))).astype(BF16)


def out_kernel(
    grad_ref, got_first_ref, got_second_ref, first_ref, second_ref, w1t_ref, sel_ref, w2_hbm, mask_ref, after_ref,
    out_ref, w2_ref, w2t_ref, v_ref, planes_ref, got_ref, own_ref, sems,
):
    (copy,) = fetch((w2_hbm,), (w2_ref,), sems)
    for x in range(8):
        planes_ref[x] = grad_ref[1, :, x * 128 : (x + 1) * 128]

    def place(j, spread):
        for x in range(8):
            v_ref[j * CH : (j + 1) * CH, (x + 1) * 128 : (x + 2) * 128] = spread[x * CH : (x + 1) * CH]

    spread_planes(planes_ref[...].reshape(8 * CH, 128), sel_ref, place)
    lower_ref, upper_ref = lower_upper(got_first_ref, got_second_ref, got_ref)
    low_ref, high_ref = lower_upper(first_ref, second_ref, own_ref)
    v_ref[:, :128] = spread_rim(beside(lower_ref, low_ref[:CH, :], True, w1t_ref), sel_ref[0])[0]
    v_ref[:, 1152:] = spread_rim(beside(upper_ref, high_ref[:CH, :], False, w1t_ref), sel_ref[2])[0]
    copy.wait()
    for d in range(3):
        w2t_ref[d * CH : (d + 1) * CH, :] = turned(w2_ref, d)
    full = dot(w2t_ref[...], v_ref[...])
    total = full[:CH, :1024] + full[CH : 2 * CH, 128:1152] + full[2 * CH :, 256:]
    total = mask_ref[...] * total
    for x in range(0, 8, 2):
        even = total[:, x * 128 : (x + 1) * 128]
        odd = total[:, (x + 1) * 128 : (x + 2) * 128]
        first, second = pair_planes(even, odd)
        out_ref[:, x * 64 : x * 64 + 128] = first.astype(BF16)
        out_ref[:, 512 + x * 64 : 640 + x * 64] = second.astype(BF16)


def core_index():
    return lax.rem(lax.axis_index("group"), 2)


def add_kernel(own_ref, got_ref, out_ref):
    out_ref[...] = (own_ref[...] + got_ref[...].astype(F32)).astype(BF16)


def rows_kernel(got_ref, after_ref, out_ref):
    total = got_ref[0].astype(F32)
    for k in range(1, AROUND):
        total += got_ref[k].astype(F32)
    out_ref[...] = total.astype(BF16)


def total_kernel(*refs):
    out_ref, slots_ref = refs[-2:]
    me = lax.rem(lax.axis_index("dev"), 8) // 2
    for k in range(4):
        slots_ref[me ^ k] = refs[k][...]
    total = slots_ref[0].astype(F32)
    for k in range(1, 4):
        total += slots_ref[k].astype(F32)
    total = total.astype(BF16)
    for k in range(AROUND):
        out_ref[k] = total


def unpack_kernel(own, *refs):
    half_ref = refs[0]
    one_hbm, two_hbm, packed_ref, out_ref, sems = refs[-5:]
    packed_ref[...] = half_ref[...].astype(F32)
    lane = lax.broadcasted_iota(jnp.int32, (CH, 128), 1)

    def block_of(block):
        d, j = block // 9, block % 9
        at, off = j * CH // 128, j * CH % 128
        row = at * 3 * CH + d * CH
        value = packed_ref[row : row + CH, :]
        if off == 0:
            return value
        value = pltpu.roll(value, 128 - off, 1)
        if off > 32:
            more = pltpu.roll(packed_ref[row + 3 * CH : row + 4 * CH, :], 128 - off, 1)
            value = jnp.where(lane < 128 - off, value, more)
        return value

    def write(hbm, make):
        copies = []
        for first in range(0, 27, 9):
            for tap in range(first, first + 9):
                out_ref[tap] = make(tap)
            part = pl.ds(first, 9)
            copies.append(pltpu.make_async_copy(out_ref.at[part], hbm.at[part], sems.at[len(copies)]))
            copies[-1].start()
        for copy in copies:
            copy.wait()

    def turned_block(tap):
        wide = jnp.concatenate([block_of(tap), jnp.zeros((32, 128), F32)], axis=0)
        return wide.T[:CH, :CH]

    core = core_index()

    @pl.when(core == (0 if own else 1))
    def _():
        write(one_hbm, turned_block)

    @pl.when(core == (1 if own else 0))
    def _():
        write(two_hbm, lambda tap: block_of(26 - tap)[:, :CH])


def shape(dims, dtype=BF16):
    return jax.ShapeDtypeStruct(dims, dtype)


def call(kernel, outs, *args, scratch=(), specs=None, out_specs=None, limit=8, flops=0, aliases=None, name=None):
    specs = specs or {}
    return pl.pallas_call(
        kernel,
        out_shape=outs,
        in_specs=[specs.get(k, VMEM) for k in range(len(args))],
        out_specs=out_specs or jax.tree.map(lambda _: VMEM, outs),
        scratch_shapes=scratch,
        input_output_aliases=aliases or {},
        compiler_params=pltpu.CompilerParams(vmem_limit_bytes=limit << 20),
        cost_estimate=pl.CostEstimate(flops=flops, bytes_accessed=1 << 20, transcendentals=0),
        name=name,
    )(*args)


def device_pairs(move):
    pairs = []
    for index in range(256):
        group, dev = index // 32, index % 32
        x, y, z, core = move(dev // 8, group // 2, dev % 8, group % 2)
        pairs.append((index, (y * 2 + core) * 32 + x * 8 + z))
    return pairs


def around_groups():
    return [
        [(y * 2 + core) * 32 + x * 8 + pair * 2 + z for y in range(4) for x in range(4) for z in range(2)]
        for core in range(2)
        for pair in range(4)
    ]


def all_to_all(value):
    return lax.all_to_all(value, BOTH, 0, 0, axis_index_groups=around_groups(), tiled=True)


def swap_core(value):
    return lax.ppermute(value, BOTH, device_pairs(lambda x, y, z, core: (x, y, z, 1 - core)))


def swap_z(value, k):
    return lax.ppermute(value, BOTH, device_pairs(lambda x, y, z, core: (x, y, z ^ (2 * k), core)))


def dev_swap(value, first):
    pairs = [(i, i + 1) for i in range(first, lax.axis_size("dev") - 1, 2)]
    return lax.ppermute(value, "dev", pairs + [(j, i) for i, j in pairs])


def in_hbm(value):
    return pltpu.with_memory_space_constraint(value, pltpu.HBM)


def per_device(features_in, occupancy, cotangent, kernel_one, kernel_two, neighbours):
    features_in = in_hbm(features_in)
    cotangent = in_hbm(cotangent)
    occ = in_hbm(occupancy.reshape(1, 1024))
    w1 = in_hbm(kernel_one.reshape(27 * CH, CH))
    w2 = in_hbm(kernel_two.reshape(27 * CH, CH))
    neighbours = in_hbm(neighbours)
    first, second = call(
        rim_kernel,
        [shape((3 * CH + 32, 128))] * 2,
        features_in, cotangent, occ, neighbours,
        specs={k: HBM for k in range(4)},
        scratch=INPUTS + [
            pltpu.SMEM((2, 27), jnp.int32), pltpu.VMEM((2, 3 * CH + 32, 128), BF16), pltpu.SemaphoreType.DMA((4,))
        ],
        name="rims",
    )
    got_first = dev_swap(first, 0)
    got_second = dev_swap(second, 1)
    v, part, w1t, wb, sel, mask = call(
        prep_kernel,
        [
            shape((2, K9, 1024)), shape((2, CH, 1024), F32),
            shape((3 * CH, K9)), shape((3 * CH, K9)), shape((3, 128, 1152)), shape((1, 1024), F32),
        ],
        features_in, cotangent, occ, w1, w2, neighbours,
        specs={k: HBM for k in range(6)},
        scratch=INPUTS + [
            pltpu.VMEM((27 * CH, CH), BF16), pltpu.VMEM((27 * CH, CH), BF16), pltpu.SMEM((2, 27), jnp.int32),
            pltpu.VMEM((8, 2 * CH, 128), BF16), pltpu.SemaphoreType.DMA((6,)),
        ],
        limit=16,
        flops=4 << 30,
        name="prep",
    )
    grad, rim = call(
        point_kernel,
        [shape((2, CH, 1024)), shape((2, K9, 256))],
        part, w1t, wb, sel, mask, got_first, got_second,
        scratch=[pltpu.VMEM((2, 3 * CH + 32, 128), BF16)],
        limit=16,
        flops=1 << 30,
        name="points",
    )

    def terms(kept):
        return call(
            functools.partial(term_kernel, kept),
            shape((HALF, 128), F32 if kept else BF16),
            v, rim, grad,
            limit=16,
            flops=2 << 30,
            name="terms_kept" if kept else "terms_sent",
        )

    got = swap_core(terms(False))
    value = call(add_kernel, shape((HALF, 128)), terms(True), got, name="sum_core")
    moved = all_to_all(value.reshape(AROUND, HALF // AROUND, 128))
    features_out = call(
        out_kernel,
        shape((CH, 1024)),
        grad, got_first, got_second, first, second, w1t, sel, w2, mask, value,
        specs={7: HBM, 9: ANY},
        scratch=[
            pltpu.VMEM((27 * CH, CH), BF16), pltpu.VMEM((3 * CH, K9), BF16),
            pltpu.VMEM((K9, 1280), BF16), pltpu.VMEM((8, CH, 128), BF16),
            pltpu.VMEM((2, 3 * CH + 32, 128), BF16), pltpu.VMEM((2, 3 * CH + 32, 128), BF16),
            pltpu.SemaphoreType.DMA((1,)),
        ],
        limit=16,
        flops=3 << 30,
        name="features",
    )
    value = call(
        rows_kernel, shape((HALF // AROUND, 128)), moved, in_hbm(features_out),
        specs={1: HBM}, name="sum_around",
    )
    arrived = [value] + [swap_z(value, k) for k in range(1, 4)]
    value = call(
        total_kernel, shape((AROUND, HALF // AROUND, 128)), *arrived,
        scratch=[pltpu.VMEM((4, HALF // AROUND, 128), BF16)],
        name="sum_z",
    )
    mine = all_to_all(value).reshape(HALF, 128)
    other = swap_core(mine)
    grads = []
    for own, half in ((True, mine), (False, other)):
        grads = call(
            functools.partial(unpack_kernel, own),
            [shape((27, CH, CH), F32)] * 2,
            half, *grads,
            specs={1: HBM, 2: HBM},
            out_specs=[HBM, HBM],
            aliases={} if own else {1: 0, 2: 1},
            scratch=[
                pltpu.VMEM((HALF, 128), F32), pltpu.VMEM((27, CH, CH), F32), pltpu.SemaphoreType.DMA((3,))
            ],
            limit=16,
            name="unpack_own" if own else "unpack_other",
        )
    kernel_one_grad, kernel_two_grad = grads
    return (features_out, kernel_one_grad, kernel_two_grad)


def solution(mesh):
    return jax.shard_map(
        per_device,
        mesh=mesh,
        in_specs=(
            P(None, ("group", "dev")),
            P(("group", "dev")),
            P(None, ("group", "dev")),
            P(),
            P(),
            P(("group", "dev"), None),
        ),
        out_specs=(P(None, ("group", "dev")), P(), P()),
        check_vma=False,
    )
```

```python
import functools

import jax
import jax.numpy as jnp
from jax import lax
from jax.experimental import pallas as pl
from jax.experimental.pallas import tpu as pltpu
from jax.sharding import PartitionSpec as P

CH = 96
PAIRS = [(dy, dz) for dy in (-1, 0, 1) for dz in (-1, 0, 1)]
K9 = 9 * CH
F32 = jnp.float32
BF16 = jnp.bfloat16
NN = (((1,), (0,)), ((), ()))
NT = (((1,), (1,)), ((), ()))
VMEM = pl.BlockSpec(memory_space=pltpu.VMEM)
SMEM = pl.BlockSpec(memory_space=pltpu.SMEM)
ANY = pl.BlockSpec(memory_space=pl.ANY)
HBM = pl.BlockSpec(memory_space=pltpu.HBM)
BOTH = ("group", "dev")
ROWS = 4096
HALF = ROWS // 2
AROUND = 32
INPUTS = [pltpu.VMEM((CH, 1024), BF16), pltpu.VMEM((CH, 1024), BF16), pltpu.VMEM((1, 1024), jnp.int32)]


def dot(a, b, dims=NN):
    return lax.dot_general(a, b, dims, preferred_element_type=F32)


def lanes_low(rows):
    return lax.broadcasted_iota(jnp.int32, (rows, 128), 1) < 64


def pair_planes(first, second):
    low = lanes_low(first.shape[0])
    even = jnp.where(low, first, pltpu.roll(second, 64, 1))
    odd = jnp.where(low, pltpu.roll(first, 64, 1), second)
    return even, odd


def to_planes(ref, x):
    first = ref[:, x * 64 : x * 64 + 128].astype(F32)
    second = ref[:, 512 + x * 64 : 640 + x * 64].astype(F32)
    return pair_planes(first, second)


def source_lanes(nb_ref, face):
    base = {0: 0, -1: 2, 1: 4}[face]
    lane = lax.broadcasted_iota(jnp.int32, (1, 128), 1)
    y = (lane // 8) % 8
    z = lane % 8
    rows = []
    for dy, dz in PAIRS:
        far_y = y + dy
        far_z = z + dz
        out_y = (far_y < 0) | (far_y > 7)
        out_z = (far_z < 0) | (far_z > 7)

        def entry(block):
            def at(sy, sz):
                return nb_ref[block, (face + 1) * 9 + (sy + 1) * 3 + sz + 1] - base

            return jnp.where(
                out_y,
                jnp.where(out_z, at(dy, dz), at(dy, 0)),
                jnp.where(out_z, at(0, dz), at(0, 0)),
            )

        found = jnp.where(lane < 64, entry(0), entry(1))
        column = found * 64 + (far_y & 7) * 8 + (far_z & 7)
        rows.append(jnp.where(found < 0, -1, column).astype(F32))
    return rows


def selection(rows):
    source = lax.broadcasted_iota(jnp.int32, (128, 128), 0).astype(F32)
    return jnp.concatenate([jnp.where(source == row, 1.0, 0.0).astype(BF16) for row in rows], axis=1)


def fetch(sources, targets, sems):
    copies = [
        pltpu.make_async_copy(source, target, sems.at[k])
        for k, (source, target) in enumerate(zip(sources, targets))
    ]
    for copy in copies:
        copy.start()
    return copies


def rim_kernel(
    feat_hbm, cot_hbm, occ_hbm, nb_hbm, first_ref, second_ref, feat_ref, cot_ref, occ_ref, nb_ref, both_ref, sems
):
    copies = fetch((nb_hbm, occ_hbm, feat_hbm, cot_hbm), (nb_ref, occ_ref, feat_ref, cot_ref), sems)
    copies[0].wait()
    inner = source_lanes(nb_ref, 0)
    sides = [inner + source_lanes(nb_ref, face) for face in (-1, 1)]
    for copy in copies[1:]:
        copy.wait()
    for x, edge, rows in ((0, 0, sides[0]), (6, 1, sides[1])):
        out_ref = both_ref.at[edge]
        masks = to_planes(occ_ref, x)
        planes = [jnp.where(m > 0, p, 0.0) for m, p in zip(masks, to_planes(feat_ref, x))]
        out_ref[:CH, :] = planes[edge].astype(BF16)
        out_ref[CH : 2 * CH, :] = jnp.where(masks[edge] > 0, to_planes(cot_ref, x)[edge], 0.0).astype(BF16)
        out_ref[2 * CH : 3 * CH, :] = planes[1 - edge].astype(BF16)
        table = jnp.concatenate([masks[edge]] + rows + [jnp.zeros((13, 128), F32)], axis=0)
        out_ref[3 * CH :, :] = table.astype(BF16)
    odd = dev_parity()
    first_ref[...] = both_ref[1 - odd]
    second_ref[...] = both_ref[odd]


def dev_parity():
    return lax.rem(lax.axis_index("dev"), 2)


def lower_upper(first_ref, second_ref, both_ref):
    both_ref[0] = first_ref[...]
    both_ref[1] = second_ref[...]
    odd = dev_parity()
    return both_ref.at[1 - odd], both_ref.at[odd]


def turned(w_ref, d):
    return w_ref[d * K9 : (d + 1) * K9, :].astype(F32).T.astype(BF16)


def prep_kernel(
    feat_hbm, cot_hbm, occ_hbm, w1_hbm, w2_hbm, nb_hbm,
    v_ref, part_ref, w1t_ref, wb_ref, sel_ref, mask_ref,
    feat_ref, cot_ref, occ_ref, w1_ref, w2_ref, nb_ref, planes_ref, sems,
):
    copies = fetch(
        (nb_hbm, occ_hbm, feat_hbm, cot_hbm, w1_hbm, w2_hbm),
        (nb_ref, occ_ref, feat_ref, cot_ref, w1_ref, w2_ref),
        sems,
    )
    copies[0].wait()
    for index, face in enumerate((-1, 0, 1)):
        sel_ref[index] = selection(source_lanes(nb_ref, face))
    for copy in copies[1:4]:
        copy.wait()
    for x in range(0, 8, 2):
        masks = to_planes(occ_ref, x)
        for k in range(2):
            mask_ref[:, (x + k) * 128 : (x + k + 1) * 128] = masks[k]
        for row, ref in ((0, feat_ref), (CH, cot_ref)):
            both = to_planes(ref, x)
            for k in range(2):
                planes_ref[x + k, row : row + CH, :] = jnp.where(masks[k] > 0, both[k], 0.0).astype(BF16)
    stacked = planes_ref[...].reshape(8 * 2 * CH, 128)

    def place(j, spread):
        for x in range(8):
            for k in range(2):
                r = (x * 2 + k) * CH
                v_ref[k, j * CH : (j + 1) * CH, x * 128 : (x + 1) * 128] = spread[r : r + CH]

    spread_planes(stacked, sel_ref, place)
    for copy in copies[4:]:
        copy.wait()
    for d in range(3):
        w1t_ref[d * CH : (d + 1) * CH, :] = turned(w1_ref, d)
        wb_ref[d * CH : (d + 1) * CH, :] = jnp.concatenate(
            [w2_ref[(26 - d * 9 - j) * CH : (27 - d * 9 - j) * CH, :] for j in range(9)], axis=1
        )
    for k, w_ref in ((0, w1t_ref), (1, wb_ref)):
        full = dot(w_ref[...], v_ref[k])
        part_ref[k] = full[CH : 2 * CH]
        part_ref[k, :, 128:] += full[:CH, :896]
        part_ref[k, :, :896] += full[2 * CH :, 128:]


def spread_planes(stacked, sel_ref, place):
    for j in range(0, 9, 2):
        wide = min(256, 1152 - j * 128)
        spread = dot(stacked, sel_ref[1, :, j * 128 : j * 128 + wide]).astype(BF16)
        for k in range(wide // 128):
            place(j + k, spread[:, k * 128 : (k + 1) * 128])


def spread_rim(rim, select):
    full = dot(rim, select).astype(BF16)
    return [
        jnp.concatenate([full[r : r + CH, j * 128 : (j + 1) * 128] for j in range(9)], axis=0)
        for r in range(0, rim.shape[0], CH)
    ]


def point_kernel(
    part_ref, w1t_ref, wb_ref, sel_ref, mask_ref, v_ref, first_ref, second_ref,
    sent_ref, grad_ref, rim_ref, both_ref,
):
    low_ref, high_ref = lower_upper(first_ref, second_ref, both_ref)
    lows = spread_rim(low_ref[: 2 * CH, :], sel_ref[0])
    highs = spread_rim(high_ref[: 2 * CH, :], sel_ref[2])
    for k in range(2):
        rim_ref[k, :, :128] = lows[k]
        rim_ref[k, :, 128:] = highs[k]

    def finish(k, w_ref):
        first = part_ref[k, :, :128] + dot(w_ref[:CH, :], lows[k])
        last = part_ref[k, :, 896:] + dot(w_ref[2 * CH :, :], highs[k])
        return mask_ref[...] * jnp.concatenate([first, part_ref[k, :, 128:896], last], axis=1)

    z = finish(0, w1t_ref)
    sigma = 1.0 / (1.0 + jnp.exp(-z))
    grad_ref[1] = (z * sigma).astype(BF16)
    ga = finish(1, wb_ref)
    grad_ref[0] = (ga * sigma * (1.0 + z * (1.0 - sigma))).astype(BF16)
    which = 1 - core_index()
    write_terms(grad_ref[which], v_ref[which], rim_ref[which], sent_ref)


def write_terms(grad, inner, rims, out_ref):
    gap = jnp.zeros((CH, 128), BF16)
    middle = jnp.concatenate(
        [
            jnp.concatenate([grad[:, 128:], gap], axis=1),
            grad,
            jnp.concatenate([gap, grad[:, :896]], axis=1),
        ],
        axis=0,
    )
    sides = jnp.concatenate(
        [
            jnp.concatenate([grad[:, :128], gap], axis=1),
            jnp.concatenate([gap, gap], axis=1),
            jnp.concatenate([gap, grad[:, 896:]], axis=1),
        ],
        axis=0,
    )
    value = (dot(middle, inner, NT) + dot(sides, rims, NT)) * (262144.0 ** -0.5)
    value = jnp.concatenate([value, jnp.zeros((3 * CH, 32), F32)], axis=1).astype(out_ref.dtype)
    for k in range(7):
        out_ref[k * 3 * CH : (k + 1) * 3 * CH, :] = value[:, k * 128 : (k + 1) * 128]
    out_ref[21 * CH :, :] = jnp.zeros((HALF - 21 * CH, 128), out_ref.dtype)


def kept_kernel(v_ref, rim_ref, grad_ref, out_ref):
    which = core_index()
    write_terms(grad_ref[which], v_ref[which], rim_ref[which], out_ref)


def beside(payload_ref, own, below, w1t_ref):
    table = payload_ref[3 * CH :, :].astype(F32)
    inner = selection([table[1 + j : 2 + j] for j in range(9)])
    across = selection([table[10 + j : 11 + j] for j in range(9)])
    (edge,) = spread_rim(payload_ref[:CH, :], inner)
    (far,) = spread_rim(payload_ref[2 * CH : 3 * CH, :], inner)
    (near,) = spread_rim(own, across)
    before, after = (far, near) if below else (near, far)
    z = dot(w1t_ref[:CH, :], before) + dot(w1t_ref[CH : 2 * CH, :], edge) + dot(w1t_ref[2 * CH :, :], after)
    z = table[:1] * z
    return (z / (1.0 + jnp.exp(-z))).astype(BF16)


def out_kernel(
    grad_ref, got_first_ref, got_second_ref, first_ref, second_ref, w1t_ref, sel_ref, w2_hbm, mask_ref, after_ref,
    out_ref, w2_ref, w2t_ref, v_ref, planes_ref, got_ref, own_ref, sems,
):
    (copy,) = fetch((w2_hbm,), (w2_ref,), sems)
    for x in range(8):
        planes_ref[x] = grad_ref[1, :, x * 128 : (x + 1) * 128]

    def place(j, spread):
        for x in range(8):
            v_ref[j * CH : (j + 1) * CH, (x + 1) * 128 : (x + 2) * 128] = spread[x * CH : (x + 1) * CH]

    spread_planes(planes_ref[...].reshape(8 * CH, 128), sel_ref, place)
    lower_ref, upper_ref = lower_upper(got_first_ref, got_second_ref, got_ref)
    low_ref, high_ref = lower_upper(first_ref, second_ref, own_ref)
    v_ref[:, :128] = spread_rim(beside(lower_ref, low_ref[:CH, :], True, w1t_ref), sel_ref[0])[0]
    v_ref[:, 1152:] = spread_rim(beside(upper_ref, high_ref[:CH, :], False, w1t_ref), sel_ref[2])[0]
    copy.wait()
    for d in range(3):
        w2t_ref[d * CH : (d + 1) * CH, :] = turned(w2_ref, d)
    full = dot(w2t_ref[...], v_ref[...])
    total = full[:CH, :1024] + full[CH : 2 * CH, 128:1152] + full[2 * CH :, 256:]
    total = mask_ref[...] * total
    for x in range(0, 8, 2):
        even = total[:, x * 128 : (x + 1) * 128]
        odd = total[:, (x + 1) * 128 : (x + 2) * 128]
        first, second = pair_planes(even, odd)
        out_ref[:, x * 64 : x * 64 + 128] = first.astype(BF16)
        out_ref[:, 512 + x * 64 : 640 + x * 64] = second.astype(BF16)


def core_index():
    return lax.rem(lax.axis_index("group"), 2)


def add_kernel(own_ref, got_ref, out_hbm, sum_ref, sems):
    copies = []
    for k in range(4):
        part = pl.ds(k * HALF // 4, HALF // 4)
        sum_ref[part, :] = (own_ref[part, :] + got_ref[part, :].astype(F32)).astype(BF16)
        copies.append(pltpu.make_async_copy(sum_ref.at[part], out_hbm.at[part], sems.at[k]))
        copies[-1].start()
    for copy in copies:
        copy.wait()


def rows_kernel(got_ref, after_ref, out_ref):
    total = got_ref[0].astype(F32)
    for k in range(1, AROUND):
        total += got_ref[k].astype(F32)
    out_ref[...] = total.astype(BF16)


def total_kernel(*refs):
    out_ref, slots_ref = refs[-2:]
    me = lax.rem(lax.axis_index("dev"), 8) // 2
    for k in range(4):
        slots_ref[me ^ k] = refs[k][...]
    total = slots_ref[0].astype(F32)
    for k in range(1, 4):
        total += slots_ref[k].astype(F32)
    total = total.astype(BF16)
    for k in range(AROUND):
        out_ref[k] = total


def unpack_kernel(own, *refs):
    half_ref = refs[0]
    one_hbm, two_hbm, out_ref, sems = refs[-4:]
    lane = lax.broadcasted_iota(jnp.int32, (CH, 128), 1)

    def block_of(block):
        d, j = block // 9, block % 9
        at, off = j * CH // 128, j * CH % 128
        row = at * 3 * CH + d * CH
        value = half_ref[row : row + CH, :]
        if off > 32:
            value = jnp.where(lane < off, half_ref[row + 3 * CH : row + 4 * CH, :], value)
        if off > 0:
            value = pltpu.roll(value, 128 - off, 1)
        return value.astype(F32)

    def write(hbm, make):
        copies = []
        for first in range(0, 27, 9):
            for tap in range(first, first + 9):
                out_ref[tap] = make(tap)
            part = pl.ds(first, 9)
            copies.append(pltpu.make_async_copy(out_ref.at[part], hbm.at[part], sems.at[len(copies)]))
            copies[-1].start()
        for copy in copies:
            copy.wait()

    def turned_block(tap):
        wide = jnp.concatenate([block_of(tap), jnp.zeros((32, 128), F32)], axis=0)
        return wide.T[:CH, :CH]

    core = core_index()

    @pl.when(core == (0 if own else 1))
    def _():
        write(one_hbm, turned_block)

    @pl.when(core == (1 if own else 0))
    def _():
        write(two_hbm, lambda tap: block_of(26 - tap)[:, :CH])


def shape(dims, dtype=BF16):
    return jax.ShapeDtypeStruct(dims, dtype)


def call(kernel, outs, *args, scratch=(), specs=None, out_specs=None, limit=8, flops=0, aliases=None, name=None):
    specs = specs or {}
    return pl.pallas_call(
        kernel,
        out_shape=outs,
        in_specs=[specs.get(k, VMEM) for k in range(len(args))],
        out_specs=out_specs or jax.tree.map(lambda _: VMEM, outs),
        scratch_shapes=scratch,
        input_output_aliases=aliases or {},
        compiler_params=pltpu.CompilerParams(vmem_limit_bytes=limit << 20),
        cost_estimate=pl.CostEstimate(flops=flops, bytes_accessed=1 << 20, transcendentals=0),
        name=name,
    )(*args)


def device_pairs(move):
    pairs = []
    for index in range(256):
        group, dev = index // 32, index % 32
        x, y, z, core = move(dev // 8, group // 2, dev % 8, group % 2)
        pairs.append((index, (y * 2 + core) * 32 + x * 8 + z))
    return pairs


def around_groups():
    return [
        [(y * 2 + core) * 32 + x * 8 + pair * 2 + z for y in range(4) for x in range(4) for z in range(2)]
        for core in range(2)
        for pair in range(4)
    ]


def all_to_all(value):
    return lax.all_to_all(value, BOTH, 0, 0, axis_index_groups=around_groups(), tiled=True)


def swap_core(value):
    return lax.ppermute(value, BOTH, device_pairs(lambda x, y, z, core: (x, y, z, 1 - core)))


def swap_z(value, k):
    return lax.ppermute(value, BOTH, device_pairs(lambda x, y, z, core: (x, y, z ^ (2 * k), core)))


def dev_swap(value, first):
    pairs = [(i, i + 1) for i in range(first, lax.axis_size("dev") - 1, 2)]
    return lax.ppermute(value, "dev", pairs + [(j, i) for i, j in pairs])


def in_hbm(value):
    return pltpu.with_memory_space_constraint(value, pltpu.HBM)


def per_device(features_in, occupancy, cotangent, kernel_one, kernel_two, neighbours):
    features_in = in_hbm(features_in)
    cotangent = in_hbm(cotangent)
    occ = in_hbm(occupancy.reshape(1, 1024))
    w1 = in_hbm(kernel_one.reshape(27 * CH, CH))
    w2 = in_hbm(kernel_two.reshape(27 * CH, CH))
    neighbours = in_hbm(neighbours)
    first, second = call(
        rim_kernel,
        [shape((3 * CH + 32, 128))] * 2,
        features_in, cotangent, occ, neighbours,
        specs={k: HBM for k in range(4)},
        scratch=INPUTS + [
            pltpu.SMEM((2, 27), jnp.int32), pltpu.VMEM((2, 3 * CH + 32, 128), BF16), pltpu.SemaphoreType.DMA((4,))
        ],
        name="rims",
    )
    got_first = dev_swap(first, 0)
    got_second = dev_swap(second, 1)
    v, part, w1t, wb, sel, mask = call(
        prep_kernel,
        [
            shape((2, K9, 1024)), shape((2, CH, 1024), F32),
            shape((3 * CH, K9)), shape((3 * CH, K9)), shape((3, 128, 1152)), shape((1, 1024), F32),
        ],
        features_in, cotangent, occ, w1, w2, neighbours,
        specs={k: HBM for k in range(6)},
        scratch=INPUTS + [
            pltpu.VMEM((27 * CH, CH), BF16), pltpu.VMEM((27 * CH, CH), BF16), pltpu.SMEM((2, 27), jnp.int32),
            pltpu.VMEM((8, 2 * CH, 128), BF16), pltpu.SemaphoreType.DMA((6,)),
        ],
        limit=16,
        flops=4 << 30,
        name="prep",
    )
    sent, grad, rim = call(
        point_kernel,
        [shape((HALF, 128)), shape((2, CH, 1024)), shape((2, K9, 256))],
        part, w1t, wb, sel, mask, v, got_first, got_second,
        scratch=[pltpu.VMEM((2, 3 * CH + 32, 128), BF16)],
        limit=16,
        flops=2 << 30,
        name="points",
    )
    got = swap_core(sent)
    kept = call(kept_kernel, shape((HALF, 128), F32), v, rim, grad, limit=16, flops=2 << 30, name="terms_kept")
    value = call(
        add_kernel, shape((HALF, 128)), kept, got,
        out_specs=HBM,
        scratch=[pltpu.VMEM((HALF, 128), BF16), pltpu.SemaphoreType.DMA((4,))],
        name="sum_core",
    )
    moved = all_to_all(value.reshape(AROUND, HALF // AROUND, 128))
    features_out = call(
        out_kernel,
        shape((CH, 1024)),
        grad, got_first, got_second, first, second, w1t, sel, w2, mask, value,
        specs={7: HBM, 9: ANY},
        scratch=[
            pltpu.VMEM((27 * CH, CH), BF16), pltpu.VMEM((3 * CH, K9), BF16),
            pltpu.VMEM((K9, 1280), BF16), pltpu.VMEM((8, CH, 128), BF16),
            pltpu.VMEM((2, 3 * CH + 32, 128), BF16), pltpu.VMEM((2, 3 * CH + 32, 128), BF16),
            pltpu.SemaphoreType.DMA((1,)),
        ],
        limit=16,
        flops=3 << 30,
        name="features",
    )
    value = call(
        rows_kernel, shape((HALF // AROUND, 128)), moved, in_hbm(features_out),
        specs={1: HBM}, name="sum_around",
    )
    arrived = [value] + [swap_z(value, k) for k in range(1, 4)]
    value = call(
        total_kernel, shape((AROUND, HALF // AROUND, 128)), *arrived,
        scratch=[pltpu.VMEM((4, HALF // AROUND, 128), BF16)],
        name="sum_z",
    )
    mine = all_to_all(value).reshape(HALF, 128)
    other = swap_core(mine)
    grads = []
    for own, half in ((True, mine), (False, other)):
        grads = call(
            functools.partial(unpack_kernel, own),
            [shape((27, CH, CH), F32)] * 2,
            half, *grads,
            specs={1: HBM, 2: HBM},
            out_specs=[HBM, HBM],
            aliases={} if own else {1: 0, 2: 1},
            scratch=[pltpu.VMEM((27, CH, CH), F32), pltpu.SemaphoreType.DMA((3,))],
            limit=16,
            name="unpack_own" if own else "unpack_other",
        )
    kernel_one_grad, kernel_two_grad = grads
    return (features_out, kernel_one_grad, kernel_two_grad)


def solution(mesh):
    return jax.shard_map(
        per_device,
        mesh=mesh,
        in_specs=(
            P(None, ("group", "dev")),
            P(("group", "dev")),
            P(None, ("group", "dev")),
            P(),
            P(),
            P(("group", "dev"), None),
        ),
        out_specs=(P(None, ("group", "dev")), P(), P()),
        check_vma=False,
    )
```

```python
import functools

import jax
import jax.numpy as jnp
from jax import lax
from jax.experimental import pallas as pl
from jax.experimental.pallas import tpu as pltpu
from jax.sharding import PartitionSpec as P

CH = 96
PAIRS = [(dy, dz) for dy in (-1, 0, 1) for dz in (-1, 0, 1)]
K9 = 9 * CH
F32 = jnp.float32
BF16 = jnp.bfloat16
NN = (((1,), (0,)), ((), ()))
NT = (((1,), (1,)), ((), ()))
VMEM = pl.BlockSpec(memory_space=pltpu.VMEM)
SMEM = pl.BlockSpec(memory_space=pltpu.SMEM)
ANY = pl.BlockSpec(memory_space=pl.ANY)
HBM = pl.BlockSpec(memory_space=pltpu.HBM)
BOTH = ("group", "dev")
ROWS = 4096
HALF = ROWS // 2
AROUND = 32
INPUTS = [pltpu.VMEM((CH, 1024), BF16), pltpu.VMEM((CH, 1024), BF16), pltpu.VMEM((1, 1024), jnp.int32)]


def dot(a, b, dims=NN):
    return lax.dot_general(a, b, dims, preferred_element_type=F32)


def lanes_low(rows):
    return lax.broadcasted_iota(jnp.int32, (rows, 128), 1) < 64


def pair_planes(first, second):
    low = lanes_low(first.shape[0])
    even = jnp.where(low, first, pltpu.roll(second, 64, 1))
    odd = jnp.where(low, pltpu.roll(first, 64, 1), second)
    return even, odd


def to_planes(ref, x):
    first = ref[:, x * 64 : x * 64 + 128].astype(F32)
    second = ref[:, 512 + x * 64 : 640 + x * 64].astype(F32)
    return pair_planes(first, second)


def source_lanes(nb_ref, face):
    base = {0: 0, -1: 2, 1: 4}[face]
    lane = lax.broadcasted_iota(jnp.int32, (1, 128), 1)
    y = (lane // 8) % 8
    z = lane % 8
    rows = []
    for dy, dz in PAIRS:
        far_y = y + dy
        far_z = z + dz
        out_y = (far_y < 0) | (far_y > 7)
        out_z = (far_z < 0) | (far_z > 7)

        def entry(block):
            def at(sy, sz):
                return nb_ref[block, (face + 1) * 9 + (sy + 1) * 3 + sz + 1] - base

            return jnp.where(
                out_y,
                jnp.where(out_z, at(dy, dz), at(dy, 0)),
                jnp.where(out_z, at(0, dz), at(0, 0)),
            )

        found = jnp.where(lane < 64, entry(0), entry(1))
        column = found * 64 + (far_y & 7) * 8 + (far_z & 7)
        rows.append(jnp.where(found < 0, -1, column).astype(F32))
    return rows


def selection(rows):
    source = lax.broadcasted_iota(jnp.int32, (128, 128), 0).astype(F32)
    return jnp.concatenate([jnp.where(source == row, 1.0, 0.0).astype(BF16) for row in rows], axis=1)


def fetch(sources, targets, sems):
    copies = [
        pltpu.make_async_copy(source, target, sems.at[k])
        for k, (source, target) in enumerate(zip(sources, targets))
    ]
    for copy in copies:
        copy.start()
    return copies


def rim_kernel(
    feat_hbm, cot_hbm, occ_hbm, nb_hbm, first_ref, second_ref, feat_ref, cot_ref, occ_ref, nb_ref, both_ref, sems
):
    copies = fetch((nb_hbm, occ_hbm, feat_hbm, cot_hbm), (nb_ref, occ_ref, feat_ref, cot_ref), sems)
    copies[0].wait()
    inner = source_lanes(nb_ref, 0)
    sides = [inner + source_lanes(nb_ref, face) for face in (-1, 1)]
    for copy in copies[1:]:
        copy.wait()
    for x, edge, rows in ((0, 0, sides[0]), (6, 1, sides[1])):
        out_ref = both_ref.at[edge]
        masks = to_planes(occ_ref, x)
        planes = [jnp.where(m > 0, p, 0.0) for m, p in zip(masks, to_planes(feat_ref, x))]
        out_ref[:CH, :] = planes[edge].astype(BF16)
        out_ref[CH : 2 * CH, :] = jnp.where(masks[edge] > 0, to_planes(cot_ref, x)[edge], 0.0).astype(BF16)
        out_ref[2 * CH : 3 * CH, :] = planes[1 - edge].astype(BF16)
        table = jnp.concatenate([masks[edge]] + rows + [jnp.zeros((13, 128), F32)], axis=0)
        out_ref[3 * CH :, :] = table.astype(BF16)
    odd = dev_parity()
    first_ref[...] = both_ref[odd]
    second_ref[...] = both_ref[1 - odd]


def dev_parity():
    return lax.rem(lax.axis_index("dev"), 2)


def lower_upper(first_ref, second_ref, both_ref):
    both_ref[0] = first_ref[...]
    both_ref[1] = second_ref[...]
    odd = dev_parity()
    return both_ref.at[odd], both_ref.at[1 - odd]


def turned(w_ref, d):
    return w_ref[d * K9 : (d + 1) * K9, :].astype(F32).T.astype(BF16)


def prep_kernel(
    feat_hbm, cot_hbm, occ_hbm, w1_hbm, w2_hbm, nb_hbm,
    v_ref, part_ref, w1t_ref, wb_ref, sel_ref, mask_ref,
    feat_ref, cot_ref, occ_ref, w1_ref, w2_ref, nb_ref, planes_ref, sems,
):
    copies = fetch(
        (nb_hbm, occ_hbm, feat_hbm, cot_hbm, w1_hbm, w2_hbm),
        (nb_ref, occ_ref, feat_ref, cot_ref, w1_ref, w2_ref),
        sems,
    )
    copies[0].wait()
    for index, face in enumerate((-1, 0, 1)):
        sel_ref[index] = selection(source_lanes(nb_ref, face))
    for copy in copies[1:4]:
        copy.wait()
    for x in range(0, 8, 2):
        masks = to_planes(occ_ref, x)
        for k in range(2):
            mask_ref[:, (x + k) * 128 : (x + k + 1) * 128] = masks[k]
        for row, ref in ((0, feat_ref), (CH, cot_ref)):
            both = to_planes(ref, x)
            for k in range(2):
                planes_ref[x + k, row : row + CH, :] = jnp.where(masks[k] > 0, both[k], 0.0).astype(BF16)
    stacked = planes_ref[...].reshape(8 * 2 * CH, 128)

    def place(j, spread):
        for x in range(8):
            for k in range(2):
                r = (x * 2 + k) * CH
                v_ref[k, j * CH : (j + 1) * CH, x * 128 : (x + 1) * 128] = spread[r : r + CH]

    spread_planes(stacked, sel_ref, place)
    for copy in copies[4:]:
        copy.wait()
    for d in range(3):
        w1t_ref[d * CH : (d + 1) * CH, :] = turned(w1_ref, d)
        wb_ref[d * CH : (d + 1) * CH, :] = jnp.concatenate(
            [w2_ref[(26 - d * 9 - j) * CH : (27 - d * 9 - j) * CH, :] for j in range(9)], axis=1
        )
    for k, w_ref in ((0, w1t_ref), (1, wb_ref)):
        full = dot(w_ref[...], v_ref[k])
        part_ref[k] = full[CH : 2 * CH]
        part_ref[k, :, 128:] += full[:CH, :896]
        part_ref[k, :, :896] += full[2 * CH :, 128:]


def spread_planes(stacked, sel_ref, place):
    for j in range(0, 9, 2):
        wide = min(256, 1152 - j * 128)
        spread = dot(stacked, sel_ref[1, :, j * 128 : j * 128 + wide]).astype(BF16)
        for k in range(wide // 128):
            place(j + k, spread[:, k * 128 : (k + 1) * 128])


def spread_rim(rim, select):
    full = dot(rim, select).astype(BF16)
    return [
        jnp.concatenate([full[r : r + CH, j * 128 : (j + 1) * 128] for j in range(9)], axis=0)
        for r in range(0, rim.shape[0], CH)
    ]


def point_kernel(
    part_ref, w1t_ref, wb_ref, sel_ref, mask_ref, v_ref, first_ref, second_ref,
    sent_ref, grad_ref, rim_ref, both_ref,
):
    low_ref, high_ref = lower_upper(first_ref, second_ref, both_ref)
    lows = spread_rim(low_ref[: 2 * CH, :], sel_ref[0])
    highs = spread_rim(high_ref[: 2 * CH, :], sel_ref[2])
    for k in range(2):
        rim_ref[k, :, :128] = lows[k]
        rim_ref[k, :, 128:] = highs[k]

    def finish(k, w_ref):
        first = part_ref[k, :, :128] + dot(w_ref[:CH, :], lows[k])
        last = part_ref[k, :, 896:] + dot(w_ref[2 * CH :, :], highs[k])
        return mask_ref[...] * jnp.concatenate([first, part_ref[k, :, 128:896], last], axis=1)

    z = finish(0, w1t_ref)
    sigma = 1.0 / (1.0 + jnp.exp(-z))
    grad_ref[1] = (z * sigma).astype(BF16)
    ga = finish(1, wb_ref)
    grad_ref[0] = (ga * sigma * (1.0 + z * (1.0 - sigma))).astype(BF16)
    which = 1 - core_index()
    write_terms(grad_ref[which], v_ref[which], rim_ref[which], sent_ref)


def write_terms(grad, inner, rims, out_ref):
    gap = jnp.zeros((CH, 128), BF16)
    middle = jnp.concatenate(
        [
            jnp.concatenate([grad[:, 128:], gap], axis=1),
            grad,
            jnp.concatenate([gap, grad[:, :896]], axis=1),
        ],
        axis=0,
    )
    sides = jnp.concatenate(
        [
            jnp.concatenate([grad[:, :128], gap], axis=1),
            jnp.concatenate([gap, gap], axis=1),
            jnp.concatenate([gap, grad[:, 896:]], axis=1),
        ],
        axis=0,
    )
    value = (dot(middle, inner, NT) + dot(sides, rims, NT)) * (262144.0 ** -0.5)
    value = jnp.concatenate([value, jnp.zeros((3 * CH, 32), F32)], axis=1).astype(out_ref.dtype)
    for k in range(7):
        out_ref[k * 3 * CH : (k + 1) * 3 * CH, :] = value[:, k * 128 : (k + 1) * 128]
    out_ref[21 * CH :, :] = jnp.zeros((HALF - 21 * CH, 128), out_ref.dtype)


def kept_kernel(v_ref, rim_ref, grad_ref, out_ref):
    which = core_index()
    write_terms(grad_ref[which], v_ref[which], rim_ref[which], out_ref)


def beside(payload_ref, own, below, w1t_ref):
    table = payload_ref[3 * CH :, :].astype(F32)
    inner = selection([table[1 + j : 2 + j] for j in range(9)])
    across = selection([table[10 + j : 11 + j] for j in range(9)])
    (edge,) = spread_rim(payload_ref[:CH, :], inner)
    (far,) = spread_rim(payload_ref[2 * CH : 3 * CH, :], inner)
    (near,) = spread_rim(own, across)
    before, after = (far, near) if below else (near, far)
    z = dot(w1t_ref[:CH, :], before) + dot(w1t_ref[CH : 2 * CH, :], edge) + dot(w1t_ref[2 * CH :, :], after)
    z = table[:1] * z
    return (z / (1.0 + jnp.exp(-z))).astype(BF16)


def out_kernel(
    grad_ref, got_first_ref, got_second_ref, first_ref, second_ref, w1t_ref, sel_ref, w2_hbm, mask_ref, after_ref,
    out_ref, w2_ref, w2t_ref, v_ref, planes_ref, got_ref, own_ref, sems,
):
    (copy,) = fetch((w2_hbm,), (w2_ref,), sems)
    for x in range(8):
        planes_ref[x] = grad_ref[1, :, x * 128 : (x + 1) * 128]

    def place(j, spread):
        for x in range(8):
            v_ref[j * CH : (j + 1) * CH, (x + 1) * 128 : (x + 2) * 128] = spread[x * CH : (x + 1) * CH]

    spread_planes(planes_ref[...].reshape(8 * CH, 128), sel_ref, place)
    lower_ref, upper_ref = lower_upper(got_first_ref, got_second_ref, got_ref)
    low_ref, high_ref = lower_upper(first_ref, second_ref, own_ref)
    v_ref[:, :128] = spread_rim(beside(lower_ref, low_ref[:CH, :], True, w1t_ref), sel_ref[0])[0]
    v_ref[:, 1152:] = spread_rim(beside(upper_ref, high_ref[:CH, :], False, w1t_ref), sel_ref[2])[0]
    copy.wait()
    for d in range(3):
        w2t_ref[d * CH : (d + 1) * CH, :] = turned(w2_ref, d)
    full = dot(w2t_ref[...], v_ref[...])
    total = full[:CH, :1024] + full[CH : 2 * CH, 128:1152] + full[2 * CH :, 256:]
    total = mask_ref[...] * total
    for x in range(0, 8, 2):
        even = total[:, x * 128 : (x + 1) * 128]
        odd = total[:, (x + 1) * 128 : (x + 2) * 128]
        first, second = pair_planes(even, odd)
        out_ref[:, x * 64 : x * 64 + 128] = first.astype(BF16)
        out_ref[:, 512 + x * 64 : 640 + x * 64] = second.astype(BF16)


def core_index():
    return lax.rem(lax.axis_index("group"), 2)


def add_kernel(own_ref, got_ref, out_hbm, sum_ref, sems):
    copies = []
    for k in range(4):
        part = pl.ds(k * HALF // 4, HALF // 4)
        sum_ref[part, :] = (own_ref[part, :] + got_ref[part, :].astype(F32)).astype(BF16)
        copies.append(pltpu.make_async_copy(sum_ref.at[part], out_hbm.at[part], sems.at[k]))
        copies[-1].start()
    for copy in copies:
        copy.wait()


def rows_kernel(got_ref, after_ref, out_ref):
    total = got_ref[0].astype(F32)
    for k in range(1, AROUND):
        total += got_ref[k].astype(F32)
    out_ref[...] = total.astype(BF16)


def total_kernel(*refs):
    out_ref, slots_ref = refs[-2:]
    me = lax.rem(lax.axis_index("dev"), 8) // 2
    for k in range(4):
        slots_ref[me ^ k] = refs[k][...]
    total = slots_ref[0].astype(F32)
    for k in range(1, 4):
        total += slots_ref[k].astype(F32)
    total = total.astype(BF16)
    for k in range(AROUND):
        out_ref[k] = total


def unpack_kernel(own, *refs):
    half_ref = refs[0]
    one_hbm, two_hbm, out_ref, sems = refs[-4:]
    lane = lax.broadcasted_iota(jnp.int32, (CH, 128), 1)

    def block_of(block):
        d, j = block // 9, block % 9
        at, off = j * CH // 128, j * CH % 128
        row = at * 3 * CH + d * CH
        value = half_ref[row : row + CH, :]
        if off > 32:
            value = jnp.where(lane < off, half_ref[row + 3 * CH : row + 4 * CH, :], value)
        if off > 0:
            value = pltpu.roll(value, 128 - off, 1)
        return value.astype(F32)

    def write(hbm, make):
        copies = []
        for first in range(0, 27, 9):
            for tap in range(first, first + 9):
                out_ref[tap] = make(tap)
            part = pl.ds(first, 9)
            copies.append(pltpu.make_async_copy(out_ref.at[part], hbm.at[part], sems.at[len(copies)]))
            copies[-1].start()
        for copy in copies:
            copy.wait()

    def turned_block(tap):
        wide = jnp.concatenate([block_of(tap), jnp.zeros((32, 128), F32)], axis=0)
        return wide.T[:CH, :CH]

    core = core_index()

    @pl.when(core == (0 if own else 1))
    def _():
        write(one_hbm, turned_block)

    @pl.when(core == (1 if own else 0))
    def _():
        write(two_hbm, lambda tap: block_of(26 - tap)[:, :CH])


def shape(dims, dtype=BF16):
    return jax.ShapeDtypeStruct(dims, dtype)


def call(kernel, outs, *args, scratch=(), specs=None, out_specs=None, limit=8, flops=0, aliases=None, name=None):
    specs = specs or {}
    return pl.pallas_call(
        kernel,
        out_shape=outs,
        in_specs=[specs.get(k, VMEM) for k in range(len(args))],
        out_specs=out_specs or jax.tree.map(lambda _: VMEM, outs),
        scratch_shapes=scratch,
        input_output_aliases=aliases or {},
        compiler_params=pltpu.CompilerParams(vmem_limit_bytes=limit << 20),
        cost_estimate=pl.CostEstimate(flops=flops, bytes_accessed=1 << 20, transcendentals=0),
        name=name,
    )(*args)


def device_pairs(move):
    pairs = []
    for index in range(256):
        group, dev = index // 32, index % 32
        x, y, z, core = move(dev // 8, group // 2, dev % 8, group % 2)
        pairs.append((index, (y * 2 + core) * 32 + x * 8 + z))
    return pairs


def around_groups():
    return [
        [(y * 2 + core) * 32 + x * 8 + pair * 2 + z for y in range(4) for x in range(4) for z in range(2)]
        for core in range(2)
        for pair in range(4)
    ]


def all_to_all(value):
    return lax.all_to_all(value, BOTH, 0, 0, axis_index_groups=around_groups(), tiled=True)


def swap_core(value):
    return lax.ppermute(value, BOTH, device_pairs(lambda x, y, z, core: (x, y, z, 1 - core)))


def swap_z(value, k):
    return lax.ppermute(value, BOTH, device_pairs(lambda x, y, z, core: (x, y, z ^ (2 * k), core)))


def dev_swap(value, first):
    pairs = [(i, i + 1) for i in range(first, lax.axis_size("dev") - 1, 2)]
    return lax.ppermute(value, "dev", pairs + [(j, i) for i, j in pairs])


def in_hbm(value):
    return pltpu.with_memory_space_constraint(value, pltpu.HBM)


def per_device(features_in, occupancy, cotangent, kernel_one, kernel_two, neighbours):
    features_in = in_hbm(features_in)
    cotangent = in_hbm(cotangent)
    occ = in_hbm(occupancy.reshape(1, 1024))
    w1 = in_hbm(kernel_one.reshape(27 * CH, CH))
    w2 = in_hbm(kernel_two.reshape(27 * CH, CH))
    neighbours = in_hbm(neighbours)
    first, second = call(
        rim_kernel,
        [shape((3 * CH + 32, 128))] * 2,
        features_in, cotangent, occ, neighbours,
        specs={k: HBM for k in range(4)},
        scratch=INPUTS + [
            pltpu.SMEM((2, 27), jnp.int32), pltpu.VMEM((2, 3 * CH + 32, 128), BF16), pltpu.SemaphoreType.DMA((4,))
        ],
        name="rims",
    )
    got_first = dev_swap(first, 1)
    got_second = dev_swap(second, 0)
    v, part, w1t, wb, sel, mask = call(
        prep_kernel,
        [
            shape((2, K9, 1024)), shape((2, CH, 1024), F32),
            shape((3 * CH, K9)), shape((3 * CH, K9)), shape((3, 128, 1152)), shape((1, 1024), F32),
        ],
        features_in, cotangent, occ, w1, w2, neighbours,
        specs={k: HBM for k in range(6)},
        scratch=INPUTS + [
            pltpu.VMEM((27 * CH, CH), BF16), pltpu.VMEM((27 * CH, CH), BF16), pltpu.SMEM((2, 27), jnp.int32),
            pltpu.VMEM((8, 2 * CH, 128), BF16), pltpu.SemaphoreType.DMA((6,)),
        ],
        limit=16,
        flops=4 << 30,
        name="prep",
    )
    sent, grad, rim = call(
        point_kernel,
        [shape((HALF, 128)), shape((2, CH, 1024)), shape((2, K9, 256))],
        part, w1t, wb, sel, mask, v, got_first, got_second,
        scratch=[pltpu.VMEM((2, 3 * CH + 32, 128), BF16)],
        limit=16,
        flops=2 << 30,
        name="points",
    )
    got = swap_core(sent)
    kept = call(kept_kernel, shape((HALF, 128), F32), v, rim, grad, limit=16, flops=2 << 30, name="terms_kept")
    value = call(
        add_kernel, shape((HALF, 128)), kept, got,
        out_specs=HBM,
        scratch=[pltpu.VMEM((HALF, 128), BF16), pltpu.SemaphoreType.DMA((4,))],
        name="sum_core",
    )
    moved = all_to_all(value.reshape(AROUND, HALF // AROUND, 128))
    features_out = call(
        out_kernel,
        shape((CH, 1024)),
        grad, got_first, got_second, first, second, w1t, sel, w2, mask, value,
        specs={7: HBM, 9: ANY},
        scratch=[
            pltpu.VMEM((27 * CH, CH), BF16), pltpu.VMEM((3 * CH, K9), BF16),
            pltpu.VMEM((K9, 1280), BF16), pltpu.VMEM((8, CH, 128), BF16),
            pltpu.VMEM((2, 3 * CH + 32, 128), BF16), pltpu.VMEM((2, 3 * CH + 32, 128), BF16),
            pltpu.SemaphoreType.DMA((1,)),
        ],
        limit=16,
        flops=3 << 30,
        name="features",
    )
    value = call(
        rows_kernel, shape((HALF // AROUND, 128)), moved, in_hbm(features_out),
        specs={1: HBM}, name="sum_around",
    )
    arrived = {k: swap_z(value, k) for k in (1, 3, 2)}
    arrived = [value] + [arrived[k] for k in (1, 2, 3)]
    value = call(
        total_kernel, shape((AROUND, HALF // AROUND, 128)), *arrived,
        scratch=[pltpu.VMEM((4, HALF // AROUND, 128), BF16)],
        name="sum_z",
    )
    mine = all_to_all(value).reshape(HALF, 128)
    other = swap_core(mine)
    grads = []
    for own, half in ((True, mine), (False, other)):
        grads = call(
            functools.partial(unpack_kernel, own),
            [shape((27, CH, CH), F32)] * 2,
            half, *grads,
            specs={1: HBM, 2: HBM},
            out_specs=[HBM, HBM],
            aliases={} if own else {1: 0, 2: 1},
            scratch=[pltpu.VMEM((27, CH, CH), F32), pltpu.SemaphoreType.DMA((3,))],
            limit=16,
            name="unpack_own" if own else "unpack_other",
        )
    kernel_one_grad, kernel_two_grad = grads
    return (features_out, kernel_one_grad, kernel_two_grad)


def solution(mesh):
    return jax.shard_map(
        per_device,
        mesh=mesh,
        in_specs=(
            P(None, ("group", "dev")),
            P(("group", "dev")),
            P(None, ("group", "dev")),
            P(),
            P(),
            P(("group", "dev"), None),
        ),
        out_specs=(P(None, ("group", "dev")), P(), P()),
        check_vma=False,
    )
```

```python
import functools

import jax
import jax.numpy as jnp
from jax import lax
from jax.experimental import pallas as pl
from jax.experimental.pallas import tpu as pltpu
from jax.sharding import PartitionSpec as P

CH = 96
PAIRS = [(dy, dz) for dy in (-1, 0, 1) for dz in (-1, 0, 1)]
K9 = 9 * CH
F32 = jnp.float32
BF16 = jnp.bfloat16
NN = (((1,), (0,)), ((), ()))
NT = (((1,), (1,)), ((), ()))
VMEM = pl.BlockSpec(memory_space=pltpu.VMEM)
SMEM = pl.BlockSpec(memory_space=pltpu.SMEM)
ANY = pl.BlockSpec(memory_space=pl.ANY)
HBM = pl.BlockSpec(memory_space=pltpu.HBM)
BOTH = ("group", "dev")
ROWS = 4096
HALF = ROWS // 2
AROUND = 32
INPUTS = [pltpu.VMEM((CH, 1024), BF16), pltpu.VMEM((CH, 1024), BF16), pltpu.VMEM((1, 1024), jnp.int32)]


def dot(a, b, dims=NN):
    return lax.dot_general(a, b, dims, preferred_element_type=F32)


def lanes_low(rows):
    return lax.broadcasted_iota(jnp.int32, (rows, 128), 1) < 64


def pair_planes(first, second):
    low = lanes_low(first.shape[0])
    even = jnp.where(low, first, pltpu.roll(second, 64, 1))
    odd = jnp.where(low, pltpu.roll(first, 64, 1), second)
    return even, odd


def to_planes(ref, x):
    first = ref[:, x * 64 : x * 64 + 128].astype(F32)
    second = ref[:, 512 + x * 64 : 640 + x * 64].astype(F32)
    return pair_planes(first, second)


def source_lanes(nb_ref, face):
    base = {0: 0, -1: 2, 1: 4}[face]
    lane = lax.broadcasted_iota(jnp.int32, (1, 128), 1)
    y = (lane // 8) % 8
    z = lane % 8
    rows = []
    for dy, dz in PAIRS:
        far_y = y + dy
        far_z = z + dz
        out_y = (far_y < 0) | (far_y > 7)
        out_z = (far_z < 0) | (far_z > 7)

        def entry(block):
            def at(sy, sz):
                return nb_ref[block, (face + 1) * 9 + (sy + 1) * 3 + sz + 1] - base

            return jnp.where(
                out_y,
                jnp.where(out_z, at(dy, dz), at(dy, 0)),
                jnp.where(out_z, at(0, dz), at(0, 0)),
            )

        found = jnp.where(lane < 64, entry(0), entry(1))
        column = found * 64 + (far_y & 7) * 8 + (far_z & 7)
        rows.append(jnp.where(found < 0, -1, column).astype(F32))
    return rows


def selection(rows):
    source = lax.broadcasted_iota(jnp.int32, (128, 128), 0).astype(F32)
    return jnp.concatenate([jnp.where(source == row, 1.0, 0.0).astype(BF16) for row in rows], axis=1)


def fetch(sources, targets, sems):
    copies = [
        pltpu.make_async_copy(source, target, sems.at[k])
        for k, (source, target) in enumerate(zip(sources, targets))
    ]
    for copy in copies:
        copy.start()
    return copies


def rim_kernel(
    feat_hbm, cot_hbm, occ_hbm, nb_hbm, first_ref, second_ref, feat_ref, cot_ref, occ_ref, nb_ref, both_ref, sems
):
    copies = fetch((nb_hbm, occ_hbm, feat_hbm, cot_hbm), (nb_ref, occ_ref, feat_ref, cot_ref), sems)
    copies[0].wait()
    inner = source_lanes(nb_ref, 0)
    sides = [inner + source_lanes(nb_ref, face) for face in (-1, 1)]
    for copy in copies[1:]:
        copy.wait()
    for x, edge, rows in ((0, 0, sides[0]), (6, 1, sides[1])):
        out_ref = both_ref.at[edge]
        masks = to_planes(occ_ref, x)
        planes = [jnp.where(m > 0, p, 0.0) for m, p in zip(masks, to_planes(feat_ref, x))]
        out_ref[:CH, :] = planes[edge].astype(BF16)
        out_ref[CH : 2 * CH, :] = jnp.where(masks[edge] > 0, to_planes(cot_ref, x)[edge], 0.0).astype(BF16)
        out_ref[2 * CH : 3 * CH, :] = planes[1 - edge].astype(BF16)
        table = jnp.concatenate([masks[edge]] + rows + [jnp.zeros((13, 128), F32)], axis=0)
        out_ref[3 * CH :, :] = table.astype(BF16)
    odd = dev_parity()
    first_ref[...] = both_ref[odd]
    second_ref[...] = both_ref[1 - odd]


def dev_parity():
    return lax.rem(lax.axis_index("dev"), 2)


def lower_upper(first_ref, second_ref, both_ref):
    both_ref[0] = first_ref[...]
    both_ref[1] = second_ref[...]
    odd = dev_parity()
    return both_ref.at[odd], both_ref.at[1 - odd]


def turned(w_ref, d):
    return w_ref[d * K9 : (d + 1) * K9, :].astype(F32).T.astype(BF16)


def prep_kernel(
    feat_hbm, cot_hbm, occ_hbm, w1_hbm, w2_hbm, nb_hbm,
    v_ref, part_ref, w1t_ref, wb_ref, sel_ref, mask_ref,
    feat_ref, cot_ref, occ_ref, w1_ref, w2_ref, nb_ref, planes_ref, sems,
):
    copies = fetch(
        (nb_hbm, occ_hbm, feat_hbm, cot_hbm, w1_hbm, w2_hbm),
        (nb_ref, occ_ref, feat_ref, cot_ref, w1_ref, w2_ref),
        sems,
    )
    copies[0].wait()
    for index, face in enumerate((-1, 0, 1)):
        sel_ref[index] = selection(source_lanes(nb_ref, face))
    for copy in copies[1:4]:
        copy.wait()
    for x in range(0, 8, 2):
        masks = to_planes(occ_ref, x)
        for k in range(2):
            mask_ref[:, (x + k) * 128 : (x + k + 1) * 128] = masks[k]
        for row, ref in ((0, feat_ref), (CH, cot_ref)):
            both = to_planes(ref, x)
            for k in range(2):
                planes_ref[x + k, row : row + CH, :] = jnp.where(masks[k] > 0, both[k], 0.0).astype(BF16)
    stacked = planes_ref[...].reshape(8 * 2 * CH, 128)

    def place(j, spread):
        for x in range(8):
            for k in range(2):
                r = (x * 2 + k) * CH
                v_ref[k, j * CH : (j + 1) * CH, x * 128 : (x + 1) * 128] = spread[r : r + CH]

    spread_planes(stacked, sel_ref, place)
    for copy in copies[4:]:
        copy.wait()
    for d in range(3):
        w1t_ref[d * CH : (d + 1) * CH, :] = turned(w1_ref, d)
        wb_ref[d * CH : (d + 1) * CH, :] = jnp.concatenate(
            [w2_ref[(26 - d * 9 - j) * CH : (27 - d * 9 - j) * CH, :] for j in range(9)], axis=1
        )
    for k, w_ref in ((0, w1t_ref), (1, wb_ref)):
        full = dot(w_ref[...], v_ref[k])
        part_ref[k] = full[CH : 2 * CH]
        part_ref[k, :, 128:] += full[:CH, :896]
        part_ref[k, :, :896] += full[2 * CH :, 128:]


def spread_planes(stacked, sel_ref, place):
    for j in range(0, 9, 2):
        wide = min(256, 1152 - j * 128)
        spread = dot(stacked, sel_ref[1, :, j * 128 : j * 128 + wide]).astype(BF16)
        for k in range(wide // 128):
            place(j + k, spread[:, k * 128 : (k + 1) * 128])


def spread_rim(rim, select):
    full = dot(rim, select).astype(BF16)
    return [
        jnp.concatenate([full[r : r + CH, j * 128 : (j + 1) * 128] for j in range(9)], axis=0)
        for r in range(0, rim.shape[0], CH)
    ]


def point_kernel(
    part_ref, w1t_ref, wb_ref, sel_ref, mask_ref, v_ref, first_ref, second_ref,
    sent_ref, grad_ref, rim_ref, both_ref,
):
    low_ref, high_ref = lower_upper(first_ref, second_ref, both_ref)
    lows = spread_rim(low_ref[: 2 * CH, :], sel_ref[0])
    highs = spread_rim(high_ref[: 2 * CH, :], sel_ref[2])
    for k in range(2):
        rim_ref[k, :, :128] = lows[k]
        rim_ref[k, :, 128:] = highs[k]

    def finish(k, w_ref):
        first = part_ref[k, :, :128] + dot(w_ref[:CH, :], lows[k])
        last = part_ref[k, :, 896:] + dot(w_ref[2 * CH :, :], highs[k])
        return mask_ref[...] * jnp.concatenate([first, part_ref[k, :, 128:896], last], axis=1)

    z = finish(0, w1t_ref)
    sigma = 1.0 / (1.0 + jnp.exp(-z))
    grad_ref[1] = (z * sigma).astype(BF16)
    ga = finish(1, wb_ref)
    grad_ref[0] = (ga * sigma * (1.0 + z * (1.0 - sigma))).astype(BF16)
    which = 1 - core_index()
    write_terms(grad_ref[which], v_ref[which], rim_ref[which], sent_ref)


def write_terms(grad, inner, rims, out_ref):
    gap = jnp.zeros((CH, 128), BF16)
    middle = jnp.concatenate(
        [
            jnp.concatenate([grad[:, 128:], gap], axis=1),
            grad,
            jnp.concatenate([gap, grad[:, :896]], axis=1),
        ],
        axis=0,
    )
    sides = jnp.concatenate(
        [
            jnp.concatenate([grad[:, :128], gap], axis=1),
            jnp.concatenate([gap, gap], axis=1),
            jnp.concatenate([gap, grad[:, 896:]], axis=1),
        ],
        axis=0,
    )
    value = (dot(middle, inner, NT) + dot(sides, rims, NT)) * (262144.0 ** -0.5)
    value = jnp.concatenate([value, jnp.zeros((3 * CH, 32), F32)], axis=1).astype(out_ref.dtype)
    for k in range(7):
        out_ref[k * 3 * CH : (k + 1) * 3 * CH, :] = value[:, k * 128 : (k + 1) * 128]
    out_ref[21 * CH :, :] = jnp.zeros((HALF - 21 * CH, 128), out_ref.dtype)


def kept_kernel(v_ref, rim_ref, grad_ref, out_ref):
    which = core_index()
    write_terms(grad_ref[which], v_ref[which], rim_ref[which], out_ref)


def beside(payload_ref, own, below, w1t_ref):
    table = payload_ref[3 * CH :, :].astype(F32)
    inner = selection([table[1 + j : 2 + j] for j in range(9)])
    across = selection([table[10 + j : 11 + j] for j in range(9)])
    (edge,) = spread_rim(payload_ref[:CH, :], inner)
    (far,) = spread_rim(payload_ref[2 * CH : 3 * CH, :], inner)
    (near,) = spread_rim(own, across)
    before, after = (far, near) if below else (near, far)
    z = dot(w1t_ref[:CH, :], before) + dot(w1t_ref[CH : 2 * CH, :], edge) + dot(w1t_ref[2 * CH :, :], after)
    z = table[:1] * z
    return (z / (1.0 + jnp.exp(-z))).astype(BF16)


def out_kernel(
    grad_ref, got_first_ref, got_second_ref, first_ref, second_ref, w1t_ref, sel_ref, w2_hbm, mask_ref, after_ref,
    out_ref, w2_ref, w2t_ref, v_ref, planes_ref, got_ref, own_ref, sems,
):
    (copy,) = fetch((w2_hbm,), (w2_ref,), sems)
    for x in range(8):
        planes_ref[x] = grad_ref[1, :, x * 128 : (x + 1) * 128]

    def place(j, spread):
        for x in range(8):
            v_ref[j * CH : (j + 1) * CH, (x + 1) * 128 : (x + 2) * 128] = spread[x * CH : (x + 1) * CH]

    spread_planes(planes_ref[...].reshape(8 * CH, 128), sel_ref, place)
    lower_ref, upper_ref = lower_upper(got_first_ref, got_second_ref, got_ref)
    low_ref, high_ref = lower_upper(first_ref, second_ref, own_ref)
    v_ref[:, :128] = spread_rim(beside(lower_ref, low_ref[:CH, :], True, w1t_ref), sel_ref[0])[0]
    v_ref[:, 1152:] = spread_rim(beside(upper_ref, high_ref[:CH, :], False, w1t_ref), sel_ref[2])[0]
    copy.wait()
    for d in range(3):
        w2t_ref[d * CH : (d + 1) * CH, :] = turned(w2_ref, d)
    full = dot(w2t_ref[...], v_ref[...])
    total = full[:CH, :1024] + full[CH : 2 * CH, 128:1152] + full[2 * CH :, 256:]
    total = mask_ref[...] * total
    for x in range(0, 8, 2):
        even = total[:, x * 128 : (x + 1) * 128]
        odd = total[:, (x + 1) * 128 : (x + 2) * 128]
        first, second = pair_planes(even, odd)
        out_ref[:, x * 64 : x * 64 + 128] = first.astype(BF16)
        out_ref[:, 512 + x * 64 : 640 + x * 64] = second.astype(BF16)


def core_index():
    return lax.rem(lax.axis_index("group"), 2)


def add_kernel(own_ref, got_ref, out_ref):
    out_ref[...] = (own_ref[...] + got_ref[...].astype(F32)).astype(BF16)


def rows_kernel(got_ref, out_ref):
    total = got_ref[0].astype(F32)
    for k in range(1, AROUND):
        total += got_ref[k].astype(F32)
    out_ref[...] = total.astype(BF16)


def total_kernel(*refs):
    out_ref, slots_ref = refs[-2:]
    me = lax.rem(lax.axis_index("dev"), 8) // 2
    for k in range(4):
        slots_ref[me ^ k] = refs[k][...]
    total = slots_ref[0].astype(F32)
    for k in range(1, 4):
        total += slots_ref[k].astype(F32)
    total = total.astype(BF16)
    for k in range(AROUND):
        out_ref[k] = total


def unpack_kernel(own, *refs):
    half_ref = refs[0]
    one_hbm, two_hbm, out_ref, sems = refs[-4:]
    lane = lax.broadcasted_iota(jnp.int32, (CH, 128), 1)

    def block_of(block):
        d, j = block // 9, block % 9
        at, off = j * CH // 128, j * CH % 128
        row = at * 3 * CH + d * CH
        value = half_ref[row : row + CH, :]
        if off > 32:
            value = jnp.where(lane < off, half_ref[row + 3 * CH : row + 4 * CH, :], value)
        if off > 0:
            value = pltpu.roll(value, 128 - off, 1)
        return value.astype(F32)

    def write(hbm, make):
        copies = []
        for first in range(0, 27, 9):
            for tap in range(first, first + 9):
                out_ref[tap] = make(tap)
            part = pl.ds(first, 9)
            copies.append(pltpu.make_async_copy(out_ref.at[part], hbm.at[part], sems.at[len(copies)]))
            copies[-1].start()
        for copy in copies:
            copy.wait()

    def turned_block(tap):
        wide = jnp.concatenate([block_of(tap), jnp.zeros((32, 128), F32)], axis=0)
        return wide.T[:CH, :CH]

    core = core_index()

    @pl.when(core == (0 if own else 1))
    def _():
        write(one_hbm, turned_block)

    @pl.when(core == (1 if own else 0))
    def _():
        write(two_hbm, lambda tap: block_of(26 - tap)[:, :CH])


def shape(dims, dtype=BF16):
    return jax.ShapeDtypeStruct(dims, dtype)


def call(kernel, outs, *args, scratch=(), specs=None, out_specs=None, limit=8, flops=0, aliases=None, name=None):
    specs = specs or {}
    return pl.pallas_call(
        kernel,
        out_shape=outs,
        in_specs=[specs.get(k, VMEM) for k in range(len(args))],
        out_specs=out_specs or jax.tree.map(lambda _: VMEM, outs),
        scratch_shapes=scratch,
        input_output_aliases=aliases or {},
        compiler_params=pltpu.CompilerParams(vmem_limit_bytes=limit << 20),
        cost_estimate=pl.CostEstimate(flops=flops, bytes_accessed=1 << 20, transcendentals=0),
        name=name,
    )(*args)


def device_pairs(move):
    pairs = []
    for index in range(256):
        group, dev = index // 32, index % 32
        x, y, z, core = move(dev // 8, group // 2, dev % 8, group % 2)
        pairs.append((index, (y * 2 + core) * 32 + x * 8 + z))
    return pairs


def around_groups():
    return [
        [(y * 2 + core) * 32 + x * 8 + pair * 2 + z for y in range(4) for x in range(4) for z in range(2)]
        for core in range(2)
        for pair in range(4)
    ]


def all_to_all(value):
    return lax.all_to_all(value, BOTH, 0, 0, axis_index_groups=around_groups(), tiled=True)


def swap_core(value):
    return lax.ppermute(value, BOTH, device_pairs(lambda x, y, z, core: (x, y, z, 1 - core)))


def swap_z(value, k):
    return lax.ppermute(value, BOTH, device_pairs(lambda x, y, z, core: (x, y, z ^ (2 * k), core)))


def dev_swap(value, first):
    pairs = [(i, i + 1) for i in range(first, lax.axis_size("dev") - 1, 2)]
    return lax.ppermute(value, "dev", pairs + [(j, i) for i, j in pairs])


def in_hbm(value):
    return pltpu.with_memory_space_constraint(value, pltpu.HBM)


def per_device(features_in, occupancy, cotangent, kernel_one, kernel_two, neighbours):
    features_in = in_hbm(features_in)
    cotangent = in_hbm(cotangent)
    occ = in_hbm(occupancy.reshape(1, 1024))
    w1 = in_hbm(kernel_one.reshape(27 * CH, CH))
    w2 = in_hbm(kernel_two.reshape(27 * CH, CH))
    neighbours = in_hbm(neighbours)
    first, second = call(
        rim_kernel,
        [shape((3 * CH + 32, 128))] * 2,
        features_in, cotangent, occ, neighbours,
        specs={k: HBM for k in range(4)},
        scratch=INPUTS + [
            pltpu.SMEM((2, 27), jnp.int32), pltpu.VMEM((2, 3 * CH + 32, 128), BF16), pltpu.SemaphoreType.DMA((4,))
        ],
        name="rims",
    )
    got_first = dev_swap(first, 1)
    got_second = dev_swap(second, 0)
    v, part, w1t, wb, sel, mask = call(
        prep_kernel,
        [
            shape((2, K9, 1024)), shape((2, CH, 1024), F32),
            shape((3 * CH, K9)), shape((3 * CH, K9)), shape((3, 128, 1152)), shape((1, 1024), F32),
        ],
        features_in, cotangent, occ, w1, w2, neighbours,
        specs={k: HBM for k in range(6)},
        scratch=INPUTS + [
            pltpu.VMEM((27 * CH, CH), BF16), pltpu.VMEM((27 * CH, CH), BF16), pltpu.SMEM((2, 27), jnp.int32),
            pltpu.VMEM((8, 2 * CH, 128), BF16), pltpu.SemaphoreType.DMA((6,)),
        ],
        limit=16,
        flops=4 << 30,
        name="prep",
    )
    sent, grad, rim = call(
        point_kernel,
        [shape((HALF, 128)), shape((2, CH, 1024)), shape((2, K9, 256))],
        part, w1t, wb, sel, mask, v, got_first, got_second,
        scratch=[pltpu.VMEM((2, 3 * CH + 32, 128), BF16)],
        limit=16,
        flops=2 << 30,
        name="points",
    )
    got = swap_core(sent)
    kept = call(kept_kernel, shape((HALF, 128), F32), v, rim, grad, limit=16, flops=2 << 30, name="terms_kept")
    value = call(add_kernel, shape((HALF, 128)), kept, got, name="sum_core")
    moved = all_to_all(value.reshape(AROUND, HALF // AROUND, 128))
    value = call(rows_kernel, shape((HALF // AROUND, 128)), moved, name="sum_around")
    arrived = {k: swap_z(value, k) for k in (1, 3, 2)}
    arrived = [value] + [arrived[k] for k in (1, 2, 3)]
    features_out = call(
        out_kernel,
        shape((CH, 1024)),
        grad, got_first, got_second, first, second, w1t, sel, w2, mask, value,
        specs={7: HBM, 9: ANY},
        scratch=[
            pltpu.VMEM((27 * CH, CH), BF16), pltpu.VMEM((3 * CH, K9), BF16),
            pltpu.VMEM((K9, 1280), BF16), pltpu.VMEM((8, CH, 128), BF16),
            pltpu.VMEM((2, 3 * CH + 32, 128), BF16), pltpu.VMEM((2, 3 * CH + 32, 128), BF16),
            pltpu.SemaphoreType.DMA((1,)),
        ],
        limit=16,
        flops=3 << 30,
        name="features",
    )
    value = call(
        total_kernel, shape((AROUND, HALF // AROUND, 128)), *arrived, in_hbm(features_out),
        specs={4: HBM},
        scratch=[pltpu.VMEM((4, HALF // AROUND, 128), BF16)],
        name="sum_z",
    )
    mine = all_to_all(value).reshape(HALF, 128)
    other = swap_core(mine)
    grads = []
    for own, half in ((True, mine), (False, other)):
        grads = call(
            functools.partial(unpack_kernel, own),
            [shape((27, CH, CH), F32)] * 2,
            half, *grads,
            specs={1: HBM, 2: HBM},
            out_specs=[HBM, HBM],
            aliases={} if own else {1: 0, 2: 1},
            scratch=[pltpu.VMEM((27, CH, CH), F32), pltpu.SemaphoreType.DMA((3,))],
            limit=16,
            name="unpack_own" if own else "unpack_other",
        )
    kernel_one_grad, kernel_two_grad = grads
    return (features_out, kernel_one_grad, kernel_two_grad)


def solution(mesh):
    return jax.shard_map(
        per_device,
        mesh=mesh,
        in_specs=(
            P(None, ("group", "dev")),
            P(("group", "dev")),
            P(None, ("group", "dev")),
            P(),
            P(),
            P(("group", "dev"), None),
        ),
        out_specs=(P(None, ("group", "dev")), P(), P()),
        check_vma=False,
    )
```

```python
import functools

import jax
import jax.numpy as jnp
from jax import lax
from jax.experimental import pallas as pl
from jax.experimental.pallas import tpu as pltpu
from jax.sharding import PartitionSpec as P

CH = 96
PAIRS = [(dy, dz) for dy in (-1, 0, 1) for dz in (-1, 0, 1)]
K9 = 9 * CH
F32 = jnp.float32
BF16 = jnp.bfloat16
NN = (((1,), (0,)), ((), ()))
NT = (((1,), (1,)), ((), ()))
VMEM = pl.BlockSpec(memory_space=pltpu.VMEM)
SMEM = pl.BlockSpec(memory_space=pltpu.SMEM)
ANY = pl.BlockSpec(memory_space=pl.ANY)
HBM = pl.BlockSpec(memory_space=pltpu.HBM)
BOTH = ("group", "dev")
ROWS = 4096
HALF = ROWS // 2
AROUND = 32
INPUTS = [pltpu.VMEM((CH, 1024), BF16), pltpu.VMEM((CH, 1024), BF16), pltpu.VMEM((1, 1024), jnp.int32)]


def dot(a, b, dims=NN):
    return lax.dot_general(a, b, dims, preferred_element_type=F32)


def lanes_low(rows):
    return lax.broadcasted_iota(jnp.int32, (rows, 128), 1) < 64


def pair_planes(first, second):
    low = lanes_low(first.shape[0])
    even = jnp.where(low, first, pltpu.roll(second, 64, 1))
    odd = jnp.where(low, pltpu.roll(first, 64, 1), second)
    return even, odd


def to_planes(ref, x):
    first = ref[:, x * 64 : x * 64 + 128].astype(F32)
    second = ref[:, 512 + x * 64 : 640 + x * 64].astype(F32)
    return pair_planes(first, second)


def source_lanes(nb_ref, face):
    base = {0: 0, -1: 2, 1: 4}[face]
    lane = lax.broadcasted_iota(jnp.int32, (1, 128), 1)
    y = (lane // 8) % 8
    z = lane % 8
    rows = []
    for dy, dz in PAIRS:
        far_y = y + dy
        far_z = z + dz
        out_y = (far_y < 0) | (far_y > 7)
        out_z = (far_z < 0) | (far_z > 7)

        def entry(block):
            def at(sy, sz):
                return nb_ref[block, (face + 1) * 9 + (sy + 1) * 3 + sz + 1] - base

            return jnp.where(
                out_y,
                jnp.where(out_z, at(dy, dz), at(dy, 0)),
                jnp.where(out_z, at(0, dz), at(0, 0)),
            )

        found = jnp.where(lane < 64, entry(0), entry(1))
        column = found * 64 + (far_y & 7) * 8 + (far_z & 7)
        rows.append(jnp.where(found < 0, -1, column).astype(F32))
    return rows


def selection(rows):
    source = lax.broadcasted_iota(jnp.int32, (128, 128), 0).astype(F32)
    return jnp.concatenate([jnp.where(source == row, 1.0, 0.0).astype(BF16) for row in rows], axis=1)


def fetch(sources, targets, sems):
    copies = [
        pltpu.make_async_copy(source, target, sems.at[k])
        for k, (source, target) in enumerate(zip(sources, targets))
    ]
    for copy in copies:
        copy.start()
    return copies


def rim_kernel(
    feat_hbm, cot_hbm, occ_hbm, nb_hbm, first_ref, second_ref, feat_ref, cot_ref, occ_ref, nb_ref, both_ref, sems
):
    copies = fetch((nb_hbm, occ_hbm, feat_hbm, cot_hbm), (nb_ref, occ_ref, feat_ref, cot_ref), sems)
    copies[0].wait()
    inner = source_lanes(nb_ref, 0)
    sides = [inner + source_lanes(nb_ref, face) for face in (-1, 1)]
    for copy in copies[1:]:
        copy.wait()
    for x, edge, rows in ((0, 0, sides[0]), (6, 1, sides[1])):
        out_ref = both_ref.at[edge]
        masks = to_planes(occ_ref, x)
        planes = [jnp.where(m > 0, p, 0.0) for m, p in zip(masks, to_planes(feat_ref, x))]
        out_ref[:CH, :] = planes[edge].astype(BF16)
        out_ref[CH : 2 * CH, :] = jnp.where(masks[edge] > 0, to_planes(cot_ref, x)[edge], 0.0).astype(BF16)
        out_ref[2 * CH : 3 * CH, :] = planes[1 - edge].astype(BF16)
        table = jnp.concatenate([masks[edge]] + rows + [jnp.zeros((13, 128), F32)], axis=0)
        out_ref[3 * CH :, :] = table.astype(BF16)
    odd = dev_parity()
    first_ref[...] = both_ref[odd]
    second_ref[...] = both_ref[1 - odd]


def dev_parity():
    return lax.rem(lax.axis_index("dev"), 2)


def lower_upper(first_ref, second_ref, both_ref):
    both_ref[0] = first_ref[...]
    both_ref[1] = second_ref[...]
    odd = dev_parity()
    return both_ref.at[odd], both_ref.at[1 - odd]


def turned(w_ref, d):
    return w_ref[d * K9 : (d + 1) * K9, :].astype(F32).T.astype(BF16)


def prep_kernel(
    feat_hbm, cot_hbm, occ_hbm, w1_hbm, w2_hbm, nb_hbm,
    v_ref, part_ref, w1t_ref, wb_ref, sel_ref, mask_ref,
    feat_ref, cot_ref, occ_ref, w1_ref, w2_ref, nb_ref, planes_ref, sems,
):
    copies = fetch(
        (nb_hbm, occ_hbm, feat_hbm, cot_hbm, w1_hbm, w2_hbm),
        (nb_ref, occ_ref, feat_ref, cot_ref, w1_ref, w2_ref),
        sems,
    )
    copies[0].wait()
    for index, face in enumerate((-1, 0, 1)):
        sel_ref[index] = selection(source_lanes(nb_ref, face))
    for copy in copies[1:4]:
        copy.wait()
    for x in range(0, 8, 2):
        masks = to_planes(occ_ref, x)
        for k in range(2):
            mask_ref[:, (x + k) * 128 : (x + k + 1) * 128] = masks[k]
        for row, ref in ((0, feat_ref), (CH, cot_ref)):
            both = to_planes(ref, x)
            for k in range(2):
                planes_ref[x + k, row : row + CH, :] = jnp.where(masks[k] > 0, both[k], 0.0).astype(BF16)
    stacked = planes_ref[...].reshape(8 * 2 * CH, 128)

    def place(j, spread):
        for x in range(8):
            for k in range(2):
                r = (x * 2 + k) * CH
                v_ref[k, j * CH : (j + 1) * CH, x * 128 : (x + 1) * 128] = spread[r : r + CH]

    spread_planes(stacked, sel_ref, place)
    for copy in copies[4:]:
        copy.wait()
    for d in range(3):
        w1t_ref[d * CH : (d + 1) * CH, :] = turned(w1_ref, d)
        wb_ref[d * CH : (d + 1) * CH, :] = jnp.concatenate(
            [w2_ref[(26 - d * 9 - j) * CH : (27 - d * 9 - j) * CH, :] for j in range(9)], axis=1
        )
    for k, w_ref in ((0, w1t_ref), (1, wb_ref)):
        full = dot(w_ref[...], v_ref[k])
        part_ref[k] = full[CH : 2 * CH]
        part_ref[k, :, 128:] += full[:CH, :896]
        part_ref[k, :, :896] += full[2 * CH :, 128:]


def spread_planes(stacked, sel_ref, place):
    for j in range(0, 9, 2):
        wide = min(256, 1152 - j * 128)
        spread = dot(stacked, sel_ref[1, :, j * 128 : j * 128 + wide]).astype(BF16)
        for k in range(wide // 128):
            place(j + k, spread[:, k * 128 : (k + 1) * 128])


def spread_rim(rim, select):
    full = dot(rim, select).astype(BF16)
    return [
        jnp.concatenate([full[r : r + CH, j * 128 : (j + 1) * 128] for j in range(9)], axis=0)
        for r in range(0, rim.shape[0], CH)
    ]


def point_kernel(
    part_ref, w1t_ref, wb_ref, sel_ref, mask_ref, v_ref, first_ref, second_ref,
    sent_ref, grad_ref, rim_ref, both_ref,
):
    low_ref, high_ref = lower_upper(first_ref, second_ref, both_ref)
    lows = spread_rim(low_ref[: 2 * CH, :], sel_ref[0])
    highs = spread_rim(high_ref[: 2 * CH, :], sel_ref[2])
    for k in range(2):
        rim_ref[k, :, :128] = lows[k]
        rim_ref[k, :, 128:] = highs[k]

    def finish(k, w_ref):
        first = part_ref[k, :, :128] + dot(w_ref[:CH, :], lows[k])
        last = part_ref[k, :, 896:] + dot(w_ref[2 * CH :, :], highs[k])
        return mask_ref[...] * jnp.concatenate([first, part_ref[k, :, 128:896], last], axis=1)

    z = finish(0, w1t_ref)
    sigma = 1.0 / (1.0 + jnp.exp(-z))
    grad_ref[1] = (z * sigma).astype(BF16)
    ga = finish(1, wb_ref)
    grad_ref[0] = (ga * sigma * (1.0 + z * (1.0 - sigma))).astype(BF16)
    which = 1 - core_index()
    write_terms(grad_ref[which], v_ref[which], rim_ref[which], sent_ref)


def write_terms(grad, inner, rims, out_ref):
    gap = jnp.zeros((CH, 128), BF16)
    middle = jnp.concatenate(
        [
            jnp.concatenate([grad[:, 128:], gap], axis=1),
            grad,
            jnp.concatenate([gap, grad[:, :896]], axis=1),
        ],
        axis=0,
    )
    sides = jnp.concatenate(
        [
            jnp.concatenate([grad[:, :128], gap], axis=1),
            jnp.concatenate([gap, gap], axis=1),
            jnp.concatenate([gap, grad[:, 896:]], axis=1),
        ],
        axis=0,
    )
    value = (dot(middle, inner, NT) + dot(sides, rims, NT)) * (262144.0 ** -0.5)
    value = jnp.concatenate([value, jnp.zeros((3 * CH, 32), F32)], axis=1).astype(out_ref.dtype)
    for k in range(7):
        out_ref[k * 3 * CH : (k + 1) * 3 * CH, :] = value[:, k * 128 : (k + 1) * 128]
    out_ref[21 * CH :, :] = jnp.zeros((HALF - 21 * CH, 128), out_ref.dtype)


def kept_kernel(v_ref, rim_ref, grad_ref, out_ref):
    which = core_index()
    write_terms(grad_ref[which], v_ref[which], rim_ref[which], out_ref)


def beside(payload_ref, own, below, w1t_ref):
    table = payload_ref[3 * CH :, :].astype(F32)
    inner = selection([table[1 + j : 2 + j] for j in range(9)])
    across = selection([table[10 + j : 11 + j] for j in range(9)])
    (edge,) = spread_rim(payload_ref[:CH, :], inner)
    (far,) = spread_rim(payload_ref[2 * CH : 3 * CH, :], inner)
    (near,) = spread_rim(own, across)
    before, after = (far, near) if below else (near, far)
    z = dot(w1t_ref[:CH, :], before) + dot(w1t_ref[CH : 2 * CH, :], edge) + dot(w1t_ref[2 * CH :, :], after)
    z = table[:1] * z
    return (z / (1.0 + jnp.exp(-z))).astype(BF16)


def out_kernel(
    grad_ref, got_first_ref, got_second_ref, first_ref, second_ref, w1t_ref, sel_ref, w2_hbm, mask_ref, after_ref,
    out_ref, w2_ref, w2t_ref, v_ref, planes_ref, got_ref, own_ref, sems,
):
    (copy,) = fetch((w2_hbm,), (w2_ref,), sems)
    for x in range(8):
        planes_ref[x] = grad_ref[1, :, x * 128 : (x + 1) * 128]

    def place(j, spread):
        for x in range(8):
            v_ref[j * CH : (j + 1) * CH, (x + 1) * 128 : (x + 2) * 128] = spread[x * CH : (x + 1) * CH]

    spread_planes(planes_ref[...].reshape(8 * CH, 128), sel_ref, place)
    lower_ref, upper_ref = lower_upper(got_first_ref, got_second_ref, got_ref)
    low_ref, high_ref = lower_upper(first_ref, second_ref, own_ref)
    v_ref[:, :128] = spread_rim(beside(lower_ref, low_ref[:CH, :], True, w1t_ref), sel_ref[0])[0]
    v_ref[:, 1152:] = spread_rim(beside(upper_ref, high_ref[:CH, :], False, w1t_ref), sel_ref[2])[0]
    copy.wait()
    for d in range(3):
        w2t_ref[d * CH : (d + 1) * CH, :] = turned(w2_ref, d)
    full = dot(w2t_ref[...], v_ref[...])
    total = full[:CH, :1024] + full[CH : 2 * CH, 128:1152] + full[2 * CH :, 256:]
    total = mask_ref[...] * total
    for x in range(0, 8, 2):
        even = total[:, x * 128 : (x + 1) * 128]
        odd = total[:, (x + 1) * 128 : (x + 2) * 128]
        first, second = pair_planes(even, odd)
        out_ref[:, x * 64 : x * 64 + 128] = first.astype(BF16)
        out_ref[:, 512 + x * 64 : 640 + x * 64] = second.astype(BF16)


def core_index():
    return lax.rem(lax.axis_index("group"), 2)


def add_kernel(own_ref, got_ref, out_hbm, sum_ref, sems):
    copies = []
    for k in range(4):
        part = pl.ds(k * HALF // 4, HALF // 4)
        sum_ref[part, :] = (own_ref[part, :] + got_ref[part, :].astype(F32)).astype(BF16)
        copies.append(pltpu.make_async_copy(sum_ref.at[part], out_hbm.at[part], sems.at[k]))
        copies[-1].start()
    for copy in copies:
        copy.wait()


def rows_kernel(got_ref, after_ref, out_ref):
    total = got_ref[0].astype(F32)
    for k in range(1, AROUND):
        total += got_ref[k].astype(F32)
    out_ref[...] = total


def pair_kernel(own_ref, got_ref, out_ref):
    out_ref[...] = own_ref[...] + got_ref[...]


def total_kernel(own_ref, got_ref, out_ref):
    total = (own_ref[...] + got_ref[...]).astype(BF16)
    for k in range(AROUND):
        out_ref[k] = total


def unpack_kernel(own, *refs):
    half_ref = refs[0]
    one_hbm, two_hbm, out_ref, sems = refs[-4:]
    lane = lax.broadcasted_iota(jnp.int32, (CH, 128), 1)

    def block_of(block):
        d, j = block // 9, block % 9
        at, off = j * CH // 128, j * CH % 128
        row = at * 3 * CH + d * CH
        value = half_ref[row : row + CH, :]
        if off > 32:
            value = jnp.where(lane < off, half_ref[row + 3 * CH : row + 4 * CH, :], value)
        if off > 0:
            value = pltpu.roll(value, 128 - off, 1)
        return value.astype(F32)

    def write(hbm, make):
        copies = []
        for first in range(0, 27, 9):
            for tap in range(first, first + 9):
                out_ref[tap] = make(tap)
            part = pl.ds(first, 9)
            copies.append(pltpu.make_async_copy(out_ref.at[part], hbm.at[part], sems.at[len(copies)]))
            copies[-1].start()
        for copy in copies:
            copy.wait()

    def turned_block(tap):
        wide = jnp.concatenate([block_of(tap), jnp.zeros((32, 128), F32)], axis=0)
        return wide.T[:CH, :CH]

    core = core_index()

    @pl.when(core == (0 if own else 1))
    def _():
        write(one_hbm, turned_block)

    @pl.when(core == (1 if own else 0))
    def _():
        write(two_hbm, lambda tap: block_of(26 - tap)[:, :CH])


def shape(dims, dtype=BF16):
    return jax.ShapeDtypeStruct(dims, dtype)


def call(kernel, outs, *args, scratch=(), specs=None, out_specs=None, limit=8, flops=0, aliases=None, name=None):
    specs = specs or {}
    return pl.pallas_call(
        kernel,
        out_shape=outs,
        in_specs=[specs.get(k, VMEM) for k in range(len(args))],
        out_specs=out_specs or jax.tree.map(lambda _: VMEM, outs),
        scratch_shapes=scratch,
        input_output_aliases=aliases or {},
        compiler_params=pltpu.CompilerParams(vmem_limit_bytes=limit << 20),
        cost_estimate=pl.CostEstimate(flops=flops, bytes_accessed=1 << 20, transcendentals=0),
        name=name,
    )(*args)


def device_pairs(move):
    pairs = []
    for index in range(256):
        group, dev = index // 32, index % 32
        x, y, z, core = move(dev // 8, group // 2, dev % 8, group % 2)
        pairs.append((index, (y * 2 + core) * 32 + x * 8 + z))
    return pairs


def around_groups():
    return [
        [(y * 2 + core) * 32 + x * 8 + pair * 2 + z for y in range(4) for x in range(4) for z in range(2)]
        for core in range(2)
        for pair in range(4)
    ]


def all_to_all(value):
    return lax.all_to_all(value, BOTH, 0, 0, axis_index_groups=around_groups(), tiled=True)


def swap_core(value):
    return lax.ppermute(value, BOTH, device_pairs(lambda x, y, z, core: (x, y, z, 1 - core)))


def swap_z(value, k):
    return lax.ppermute(value, BOTH, device_pairs(lambda x, y, z, core: (x, y, z ^ (2 * k), core)))


def dev_swap(value, first):
    pairs = [(i, i + 1) for i in range(first, lax.axis_size("dev") - 1, 2)]
    return lax.ppermute(value, "dev", pairs + [(j, i) for i, j in pairs])


def in_hbm(value):
    return pltpu.with_memory_space_constraint(value, pltpu.HBM)


def per_device(features_in, occupancy, cotangent, kernel_one, kernel_two, neighbours):
    features_in = in_hbm(features_in)
    cotangent = in_hbm(cotangent)
    occ = in_hbm(occupancy.reshape(1, 1024))
    w1 = in_hbm(kernel_one.reshape(27 * CH, CH))
    w2 = in_hbm(kernel_two.reshape(27 * CH, CH))
    neighbours = in_hbm(neighbours)
    first, second = call(
        rim_kernel,
        [shape((3 * CH + 32, 128))] * 2,
        features_in, cotangent, occ, neighbours,
        specs={k: HBM for k in range(4)},
        scratch=INPUTS + [
            pltpu.SMEM((2, 27), jnp.int32), pltpu.VMEM((2, 3 * CH + 32, 128), BF16), pltpu.SemaphoreType.DMA((4,))
        ],
        name="rims",
    )
    got_first = dev_swap(first, 1)
    got_second = dev_swap(second, 0)
    v, part, w1t, wb, sel, mask = call(
        prep_kernel,
        [
            shape((2, K9, 1024)), shape((2, CH, 1024), F32),
            shape((3 * CH, K9)), shape((3 * CH, K9)), shape((3, 128, 1152)), shape((1, 1024), F32),
        ],
        features_in, cotangent, occ, w1, w2, neighbours,
        specs={k: HBM for k in range(6)},
        scratch=INPUTS + [
            pltpu.VMEM((27 * CH, CH), BF16), pltpu.VMEM((27 * CH, CH), BF16), pltpu.SMEM((2, 27), jnp.int32),
            pltpu.VMEM((8, 2 * CH, 128), BF16), pltpu.SemaphoreType.DMA((6,)),
        ],
        limit=16,
        flops=4 << 30,
        name="prep",
    )
    sent, grad, rim = call(
        point_kernel,
        [shape((HALF, 128)), shape((2, CH, 1024)), shape((2, K9, 256))],
        part, w1t, wb, sel, mask, v, got_first, got_second,
        scratch=[pltpu.VMEM((2, 3 * CH + 32, 128), BF16)],
        limit=16,
        flops=2 << 30,
        name="points",
    )
    got = swap_core(sent)
    kept = call(kept_kernel, shape((HALF, 128), F32), v, rim, grad, limit=16, flops=2 << 30, name="terms_kept")
    value = call(
        add_kernel, shape((HALF, 128)), kept, got,
        out_specs=HBM,
        scratch=[pltpu.VMEM((HALF, 128), BF16), pltpu.SemaphoreType.DMA((4,))],
        name="sum_core",
    )
    moved = all_to_all(value.reshape(AROUND, HALF // AROUND, 128))
    features_out = call(
        out_kernel,
        shape((CH, 1024)),
        grad, got_first, got_second, first, second, w1t, sel, w2, mask, value,
        specs={7: HBM, 9: ANY},
        scratch=[
            pltpu.VMEM((27 * CH, CH), BF16), pltpu.VMEM((3 * CH, K9), BF16),
            pltpu.VMEM((K9, 1280), BF16), pltpu.VMEM((8, CH, 128), BF16),
            pltpu.VMEM((2, 3 * CH + 32, 128), BF16), pltpu.VMEM((2, 3 * CH + 32, 128), BF16),
            pltpu.SemaphoreType.DMA((1,)),
        ],
        limit=16,
        flops=3 << 30,
        name="features",
    )
    value = call(
        rows_kernel, shape((HALF // AROUND, 128), F32), moved, in_hbm(features_out),
        specs={1: HBM}, name="sum_around",
    )
    value = call(pair_kernel, shape((HALF // AROUND, 128), F32), value, swap_z(value, 1), name="sum_pair")
    value = call(
        total_kernel, shape((AROUND, HALF // AROUND, 128)), value, swap_z(value, 3), name="sum_z"
    )
    mine = all_to_all(value).reshape(HALF, 128)
    other = swap_core(mine)
    grads = []
    for own, half in ((True, mine), (False, other)):
        grads = call(
            functools.partial(unpack_kernel, own),
            [shape((27, CH, CH), F32)] * 2,
            half, *grads,
            specs={1: HBM, 2: HBM},
            out_specs=[HBM, HBM],
            aliases={} if own else {1: 0, 2: 1},
            scratch=[pltpu.VMEM((27, CH, CH), F32), pltpu.SemaphoreType.DMA((3,))],
            limit=16,
            name="unpack_own" if own else "unpack_other",
        )
    kernel_one_grad, kernel_two_grad = grads
    return (features_out, kernel_one_grad, kernel_two_grad)


def solution(mesh):
    return jax.shard_map(
        per_device,
        mesh=mesh,
        in_specs=(
            P(None, ("group", "dev")),
            P(("group", "dev")),
            P(None, ("group", "dev")),
            P(),
            P(),
            P(("group", "dev"), None),
        ),
        out_specs=(P(None, ("group", "dev")), P(), P()),
        check_vma=False,
    )
```
